32 devices in a mesh: dp: 2 (over x), ctx: 4 (over y, core), uly: 4 (over z).
Axes of the slice: x: 2, y: 2, z: 4, core: 2. Of those that a mesh axis runs over, the one named last changes fastest.
Arguments:
- queries: bfloat16 [2, 3072, 1536], P('dp', ('ctx', 'uly')), may hold values from -4.5 to 4.5
- key_rows: bfloat16 [2, 3072, 1536], P('dp', ('ctx', 'uly')), may hold values from -4.5 to 4.5
- value_rows: bfloat16 [2, 3072, 1536], P('dp', ('ctx', 'uly')), may hold values from -5 to 5
- out_grad: bfloat16 [2, 3072, 3072], P('dp', 'ctx'), may hold values from -6 to 6
- out_weight: bfloat16 [1536, 3072], P('uly'), may hold values from -0.15625 to 0.15625
- tile_lists: int32 [8, 6], replicated, may hold values from -1 to 7, as said below
- windows: int32 [12, 2], replicated, may hold values from 0 to 1, as said below
Outputs:
- query_grad: bfloat16 [2, 3072, 1536], P('dp', ('ctx', 'uly'))
- key_grad: bfloat16 [2, 3072, 1536], P('dp', ('ctx', 'uly'))
- value_grad: bfloat16 [2, 3072, 1536], P('dp', ('ctx', 'uly'))
- weight_grad: bfloat16 [1536, 3072], P('uly')
The draws below stay inside these ranges and needn't reach their ends.
Inputs may be any that keep to these rules, and one draw needn't show every extreme that they name: `tile_lists`: entry j of row Q = f * 2 + s is -1 or (f + j // 2 - 1) * 2 + j % 2; it is -1 wherever f + j // 2 - 1 lies outside 0 to 3, and never at an in-range entry with j % 2 == s. Of any two consecutive heads, at least one has windows[h, 0] = 1.
All inputs are finite; a program needn't handle non-finite values.
Results may differ from the reference program's by a relative error of at most 0.014.
Values may be sent and summed in bfloat16 or wider, within the bound.
A program may use at most 192 MiB of HBM per device.

```python
import jax
import jax.numpy as jnp
from jax import lax

HEADS = 12
HD = 128
DOUT = 3072
TILE = 384
TW = 2
NFT = 4
QTILES = 8
CT = 3072
CLIPS = 2


def drawn_pair(key):
    base_key = jax.random.fold_in(key, 7)
    sub_keys = jax.random.split(base_key, 2)
    full_shape = (CLIPS, CT, HEADS * HD)
    query_out = jnp.clip(jax.random.normal(sub_keys[0], full_shape, jnp.float32), -4.5, 4.5)
    key_out = jnp.clip(jax.random.normal(sub_keys[1], full_shape, jnp.float32), -4.5, 4.5)
    return (query_out, key_out)


def draw_queries(key, part):
    return drawn_pair(key)[0].astype(jnp.bfloat16)


def draw_key_rows(key, part):
    return drawn_pair(key)[1].astype(jnp.bfloat16)


def draw_tile_lists(key, part):
    keep_key = jax.random.fold_in(key, 11)
    slot_ids = jnp.arange(3 * TW, dtype=jnp.int32)
    slot_time = slot_ids // TW - 1
    slot_space = slot_ids % TW
    tile_ids = jnp.arange(QTILES, dtype=jnp.int32)
    frame_of = tile_ids // TW
    spot_of = tile_ids % TW
    frame_to = frame_of[:, None] + slot_time[None, :]
    inside = (frame_to >= 0) & (frame_to < NFT)
    coin = jax.random.randint(keep_key, (QTILES, 3 * TW), 0, 2) == 1
    kept = coin | (slot_space[None, :] == spot_of[:, None])
    return jnp.where(inside & kept, frame_to * TW + slot_space[None, :], -1).astype(jnp.int32)


def draw_windows(key, part):
    sub_keys = jax.random.split(jax.random.fold_in(key, 23), 4)
    head_ids = jnp.arange(HEADS, dtype=jnp.int32)
    parity = jax.random.randint(sub_keys[0], (), 0, 2)
    time_bits = jax.random.randint(sub_keys[1], (HEADS,), 0, 2)
    first_free = 1 - parity
    temporal = jnp.where((head_ids + parity) % 2 == 0, 1, jnp.where(head_ids == first_free, 0, time_bits))
    zero_at = jax.random.randint(sub_keys[2], (), 0, HEADS)
    space_bits = jax.random.randint(sub_keys[3], (HEADS,), 0, 2)
    spatial = jnp.where(head_ids == zero_at, 0, jnp.where(head_ids == (zero_at + 1) % HEADS, 1, space_bits))
    return jnp.stack([temporal, spatial], axis=1).astype(jnp.int32)


def steps_of(rng, dims, cuts, least, top_value):
    gain, own = 1.0, jax.random.fold_in(rng, 6)
    for dim, blocks in cuts:
        steps = jnp.exp(jax.random.uniform(jax.random.fold_in(own, dim), (blocks,), jnp.float32, least / len(cuts), top_value / len(cuts)))
        gain = gain * jnp.repeat(steps, dims[dim] // blocks).reshape([-1 if axis == dim else 1 for axis in range(len(dims))])
    return gain


def centred(own_key, extent, deviation, most, cuts=(), kind=jnp.bfloat16):
    drawn = jax.random.normal(own_key, extent, jnp.float32) * deviation
    if len(cuts) > 0:
        drawn = steps_of(own_key, extent, cuts, -0.22, 0.18) * drawn
    return jnp.clip(drawn, min=-most, max=most).astype(kind)


def setup_inputs(seed: int = 0) -> dict:
    streams_of = jax.random.split(jax.random.key(seed), 8)
    queries = draw_queries(jax.random.fold_in(streams_of[7], 71), 0)
    key_rows = draw_key_rows(jax.random.fold_in(streams_of[7], 71), 0)
    value_rows = centred(streams_of[2], (CLIPS, CT, HEADS * HD), 1.0, 5.0, ((0, 2), (1, 16)))
    out_grad = centred(streams_of[3], (CLIPS, CT, DOUT), 1.0, 6.0, ((0, 2), (1, 4)))
    out_weight = centred(streams_of[4], (HEADS * HD, DOUT), (HEADS * HD) ** -0.5, 0.15625, ((0, 4),))
    tile_lists = draw_tile_lists(jax.random.fold_in(streams_of[7], 71), 0)
    windows = draw_windows(jax.random.fold_in(streams_of[7], 71), 0)
    return {"queries": queries, "key_rows": key_rows, "value_rows": value_rows, "out_grad": out_grad, "out_weight": out_weight, "tile_lists": tile_lists, "windows": windows}


def cross_rounded(parts):
    lowered = lax.optimization_barrier(parts.astype(jnp.bfloat16)).astype(jnp.float32)
    return jnp.concatenate([lowered[0:1], parts[1:2], lowered[2:3]], axis=0)


def softmax_block(query_tile, key_window, allow):
    scaling = HD ** -0.5
    score_grid = (jnp.dot(query_tile, key_window.T, preferred_element_type=jnp.float32) * scaling).reshape(TW, TILE, 3 * TW, TILE)
    key_mask = allow[:, None, :, None]
    row_max = jnp.max(jnp.where(key_mask, score_grid, -jnp.inf), axis=(2, 3), keepdims=True)
    raised = jnp.where(key_mask, jnp.exp(score_grid - row_max), 0.0)
    totals = jnp.sum(raised, axis=(2, 3), keepdims=True)
    return (raised / totals).reshape(TW * TILE, 3 * TW * TILE)


def block_pass(query_tile, key_window, value_window, grad_tile, allow):
    scaling = HD ** -0.5
    mixing = softmax_block(query_tile, key_window, allow)
    mixing_low = mixing.astype(jnp.bfloat16)
    out_low = jnp.dot(mixing_low, value_window, preferred_element_type=jnp.float32).astype(jnp.bfloat16)
    row_delta = jnp.sum(out_low.astype(jnp.float32) * grad_tile.astype(jnp.float32), axis=1, keepdims=True)
    value_part = jnp.dot(mixing_low.T, grad_tile, preferred_element_type=jnp.float32)
    prob_grad = jnp.dot(grad_tile, value_window.T, preferred_element_type=jnp.float32)
    score_grad = (mixing * (prob_grad - row_delta) * scaling).astype(jnp.bfloat16)
    query_part = jnp.dot(score_grad, key_window, preferred_element_type=jnp.float32)
    key_part = jnp.dot(score_grad.T, query_tile, preferred_element_type=jnp.float32)
    return out_low, query_part, key_part, value_part


def head_pass(query_head, key_head, value_head, grad_head, allow_head):
    layer_rows = TW * TILE
    zero_frame = jnp.zeros((1, layer_rows, HD), jnp.bfloat16)
    key_padded = jnp.concatenate([zero_frame, key_head, zero_frame], axis=0)
    value_padded = jnp.concatenate([zero_frame, value_head, zero_frame], axis=0)

    def frame_step(carried, frame_at):
        key_total, value_total = carried
        key_window = lax.dynamic_slice_in_dim(key_padded, frame_at, 3, 0).reshape(3 * layer_rows, HD)
        value_window = lax.dynamic_slice_in_dim(value_padded, frame_at, 3, 0).reshape(3 * layer_rows, HD)
        query_tile = lax.dynamic_index_in_dim(query_head, frame_at, 0, keepdims=False)
        grad_tile = lax.dynamic_index_in_dim(grad_head, frame_at, 0, keepdims=False)
        allow = lax.dynamic_index_in_dim(allow_head, frame_at, 0, keepdims=False)
        out_low, query_part, key_part, value_part = block_pass(query_tile, key_window, value_window, grad_tile, allow)
        key_terms = cross_rounded(key_part.reshape(3, layer_rows, HD))
        value_terms = cross_rounded(value_part.reshape(3, layer_rows, HD))
        key_total = lax.dynamic_update_slice_in_dim(key_total, lax.dynamic_slice_in_dim(key_total, frame_at, 3, 0) + key_terms, frame_at, 0)
        value_total = lax.dynamic_update_slice_in_dim(value_total, lax.dynamic_slice_in_dim(value_total, frame_at, 3, 0) + value_terms, frame_at, 0)
        return (key_total, value_total), (out_low, query_part.astype(jnp.bfloat16))

    start_totals = jnp.zeros((NFT + 2, layer_rows, HD), jnp.float32)
    finals, stacked = lax.scan(frame_step, (start_totals, start_totals), jnp.arange(NFT, dtype=jnp.int32))
    key_total, value_total = finals
    outputs, query_grads = stacked
    return outputs, query_grads, key_total[1:-1].astype(jnp.bfloat16), value_total[1:-1].astype(jnp.bfloat16)


def reference(queries, key_rows, value_rows, out_grad, out_weight, tile_lists, windows):
    layer_rows = TW * TILE
    slot_ids = jnp.arange(3 * TW, dtype=jnp.int32)
    slot_time = slot_ids // TW - 1
    slot_space = slot_ids % TW
    tile_ids = jnp.arange(QTILES, dtype=jnp.int32)
    frame_of = tile_ids // TW
    spot_of = tile_ids % TW
    target = (frame_of[:, None] + slot_time[None, :]) * TW + slot_space[None, :]
    listed = (tile_lists == target) & (tile_lists >= 0)
    near_time = jnp.abs(slot_time)[None, None, :] <= windows[:, 0][:, None, None]
    near_space = jnp.abs(slot_space[None, :] - spot_of[:, None])[None, :, :] <= windows[:, 1][:, None, None]
    allowed = (listed[None] & near_time & near_space).reshape(HEADS, NFT, TW, 3 * TW)

    def head_view(token_rows):
        return token_rows.reshape(NFT, layer_rows, HEADS, HD).transpose(2, 0, 1, 3)

    def token_view(per_head):
        return per_head.transpose(1, 2, 0, 3).reshape(CT, HEADS * HD)

    def head_call(head_items):
        return head_pass(*head_items)

    def clip_step(grand_total, clip_items):
        query_clip, key_clip, value_clip, grad_clip = clip_items
        grad_out = jnp.dot(grad_clip, out_weight.T, preferred_element_type=jnp.float32).astype(jnp.bfloat16)
        outputs, query_grads, key_grads, value_grads = lax.map(head_call, (head_view(query_clip), head_view(key_clip), head_view(value_clip), head_view(grad_out), allowed))
        attended = token_view(outputs)
        grand_total = grand_total + jnp.dot(attended.T, grad_clip, preferred_element_type=jnp.float32)
        return grand_total, (token_view(query_grads), token_view(key_grads), token_view(value_grads))

    start_total = jnp.zeros((HEADS * HD, DOUT), jnp.float32)
    grand_total, grads = lax.scan(clip_step, start_total, (queries, key_rows, value_rows, out_grad))
    query_grad, key_grad, value_grad = grads
    return query_grad, key_grad, value_grad, (grand_total / CLIPS).astype(jnp.bfloat16)
```

```python
import functools

import jax
import jax.numpy as jnp
from jax import lax
from jax.experimental import pallas as pl
from jax.experimental.pallas import tpu as pltpu
from jax.sharding import PartitionSpec as P

HEADS = 12
HD = 128
TILE = 384
TW = 2
SLOTS = 3 * TW
LAYER = TW * TILE
MESH = pl.DeviceIdType.MESH
LOG2E = 1.4426950408889634
VMEM_LIMIT = 56 * 1024 * 1024


def head_cols(at):
    return pl.ds(pl.multiple_of(at * HD, HD), HD)


def row_block(start, rows):
    return pl.ds(pl.multiple_of(start, rows), rows)


def greet(n_uly, n_ctx, uly_at, ctx_at):
    barrier = pltpu.get_barrier_semaphore()
    for step in range(1, n_uly):
        peer = lax.rem(uly_at + step, n_uly)
        pl.semaphore_signal(barrier, inc=1, device_id={"uly": peer}, device_id_type=MESH)

    @pl.when(ctx_at > 0)
    def _():
        pl.semaphore_signal(barrier, inc=1, device_id={"ctx": ctx_at - 1}, device_id_type=MESH)

    @pl.when(ctx_at < n_ctx - 1)
    def _():
        pl.semaphore_signal(barrier, inc=1, device_id={"ctx": ctx_at + 1}, device_id_type=MESH)

    interior = jnp.logical_and(ctx_at > 0, ctx_at < n_ctx - 1)
    pl.semaphore_wait(barrier, n_uly + interior.astype(jnp.int32))


def in_kernel(n_uly, n_ctx, heads, q, k, v, og, ow, qh, kw, vw, g,
              og_v, ow_v, load_sem, own_sem, send_sem, recv_sem, halo_send, halo_recv):
    uly_at, ctx_at = lax.axis_index("uly"), lax.axis_index("ctx")
    rows = q.shape[0]
    loads = [pltpu.make_async_copy(og, og_v, load_sem.at[0]),
             pltpu.make_async_copy(ow, ow_v, load_sem.at[1])]
    for load in loads:
        load.start()
    triples = ((k, kw, LAYER), (v, vw, LAYER), (q, qh, 0))
    own = {}
    for h in range(heads):
        for i, (src, dst, base) in enumerate(triples):
            own[h, i] = pltpu.make_async_copy(
                src.at[:, head_cols(uly_at * heads + h)],
                dst.at[h, row_block(base + uly_at * rows, rows)],
                own_sem.at[h, i])
            own[h, i].start()
    greet(n_uly, n_ctx, uly_at, ctx_at)

    def piece(h, i, step, owner):
        src, dst, base = triples[i]
        peer = lax.rem(uly_at + step, n_uly)
        return pltpu.make_async_remote_copy(
            src_ref=src.at[:, head_cols(peer * heads + h)],
            dst_ref=dst.at[h, row_block(base + owner * rows, rows)],
            send_sem=send_sem.at[h, i, step - 1],
            recv_sem=recv_sem.at[h, i, step - 1],
            device_id={"uly": peer}, device_id_type=MESH)

    order = [(h, i) for h in range(heads) for i in range(2)] + [(h, 2) for h in range(heads)]
    for h, i in order:
        for step in range(1, n_uly):
            piece(h, i, step, uly_at).start()

    for load in loads:
        load.wait()

    def grad_rows(at, carry):
        chunk = row_block(at * TILE, TILE)
        out = lax.dot_general(og_v[chunk, :], ow_v[...], (((1,), (1,)), ((), ())),
                              preferred_element_type=jnp.float32).astype(jnp.bfloat16)
        for h in range(heads):
            g[h, chunk, :] = out[:, h * HD:(h + 1) * HD]
        return carry

    lax.fori_loop(0, TW, grad_rows, 0)

    def arrived(h, i):
        own[h, i].wait()
        for step in range(1, n_uly):
            owner = lax.rem(uly_at + n_uly - step, n_uly)
            piece(h, i, step, owner).wait_recv()

    def halo(h, i, side):
        buf = triples[i][1]
        slot = 2 if side == 0 else 0
        return pltpu.make_async_remote_copy(
            src_ref=buf.at[h, pl.ds(LAYER, LAYER)],
            dst_ref=buf.at[h, pl.ds(slot * LAYER, LAYER)],
            send_sem=halo_send.at[h, i, side],
            recv_sem=halo_recv.at[h, i, side],
            device_id={"ctx": ctx_at - 1 if side == 0 else ctx_at + 1}, device_id_type=MESH)

    for h in range(heads):
        for i in range(2):
            arrived(h, i)

            @pl.when(ctx_at > 0)
            def _():
                halo(h, i, 0).start()

            @pl.when(ctx_at < n_ctx - 1)
            def _():
                halo(h, i, 1).start()

    for h in range(heads):
        arrived(h, 2)
    for h in range(heads):
        for i in range(2):
            @pl.when(ctx_at > 0)
            def _():
                halo(h, i, 0).wait_send()
                halo(h, i, 1).wait_recv()

            @pl.when(ctx_at < n_ctx - 1)
            def _():
                halo(h, i, 1).wait_send()
                halo(h, i, 0).wait_recv()
    for h, i in order:
        for step in range(1, n_uly):
            piece(h, i, step, uly_at).wait_send()


def gather_heads(q, k, v, og, ow, n_uly, n_ctx, heads):
    span = LAYER
    anywhere = pl.BlockSpec(memory_space=pl.ANY)
    return pl.pallas_call(
        functools.partial(in_kernel, n_uly, n_ctx, heads),
        out_shape=(jax.ShapeDtypeStruct((heads, span, HD), jnp.bfloat16),
                   jax.ShapeDtypeStruct((heads, 3 * span, HD), jnp.bfloat16),
                   jax.ShapeDtypeStruct((heads, 3 * span, HD), jnp.bfloat16),
                   jax.ShapeDtypeStruct((heads, span, HD), jnp.bfloat16)),
        in_specs=[anywhere] * 5,
        out_specs=(anywhere, anywhere, anywhere, pl.BlockSpec(memory_space=pltpu.VMEM)),
        scratch_shapes=[
            pltpu.VMEM(og.shape, jnp.bfloat16),
            pltpu.VMEM(ow.shape, jnp.bfloat16),
            pltpu.SemaphoreType.DMA((2,)),
            pltpu.SemaphoreType.DMA((heads, 3)),
            pltpu.SemaphoreType.DMA((heads, 3, n_uly - 1)),
            pltpu.SemaphoreType.DMA((heads, 3, n_uly - 1)),
            pltpu.SemaphoreType.DMA((heads, 2, 2)),
            pltpu.SemaphoreType.DMA((heads, 2, 2)),
        ],
        compiler_params=pltpu.CompilerParams(
            collective_id=0, has_side_effects=True, vmem_limit_bytes=VMEM_LIMIT),
        name="gather_heads",
    )(q, k, v, og, ow)


def lane_fold(x, op):
    out = x[:, 0:HD]
    for at in range(HD, x.shape[1], HD):
        out = op(out, x[:, at:at + HD])
    return out


def attend_kernel(allow, q, kw, vw, g, og, dq, own, edge, wpart,
                  s_buf, p_buf, m_buf, l_buf, o_buf, dq_buf, dk_buf, dv_buf, att):
    head = pl.program_id(0)
    scaling = HD ** (-0.5)
    dk_buf[...] = jnp.zeros_like(dk_buf)
    dv_buf[...] = jnp.zeros_like(dv_buf)
    nt = (((1,), (1,)), ((), ()))
    tn = (((0,), (0,)), ((), ()))

    def query_tile(spot, carry):
        rows = row_block(spot * TILE, TILE)
        flags = (head * TW + spot) * SLOTS

        def each(body):
            def step(slot, c):
                @pl.when(allow[flags + slot] > 0)
                def _():
                    body(slot, row_block(slot * TILE, TILE))
                return c
            lax.fori_loop(0, SLOTS, step, 0)

        m_buf[...] = jnp.full_like(m_buf, -jnp.inf)
        l_buf[...] = jnp.zeros_like(l_buf)
        o_buf[...] = jnp.zeros_like(o_buf)
        dq_buf[...] = jnp.zeros_like(dq_buf)

        def score(slot, keys):
            s = lax.dot_general(q[0, rows, :], kw[0, keys, :], nt, preferred_element_type=jnp.float32)
            s_buf[slot] = s
            m_buf[...] = jnp.maximum(m_buf[...], lane_fold(s, jnp.maximum))

        each(score)
        top = jnp.max(m_buf[...], axis=1, keepdims=True)

        def weigh(slot, keys):
            p = jnp.exp2((s_buf[slot] - top) * (scaling * LOG2E))
            l_buf[...] += lane_fold(p, jnp.add)
            low = p.astype(jnp.bfloat16)
            p_buf[slot] = low
            o_buf[...] += jnp.dot(low, vw[0, keys, :], preferred_element_type=jnp.float32)

        each(weigh)
        inv = 1.0 / jnp.sum(l_buf[...], axis=1, keepdims=True)
        out = o_buf[...] * inv
        att[rows, :] = out.astype(jnp.bfloat16)
        gp = (g[0, rows, :].astype(jnp.float32) * inv).astype(jnp.bfloat16)
        delta = jnp.sum(out * gp.astype(jnp.float32), axis=1, keepdims=True)

        def back(slot, keys):
            low = p_buf[slot]
            dp = lax.dot_general(gp, vw[0, keys, :], nt, preferred_element_type=jnp.float32)
            ds = (low.astype(jnp.float32) * (dp - delta)).astype(jnp.bfloat16)
            dv_buf[keys, :] += lax.dot_general(low, gp, tn, preferred_element_type=jnp.float32)
            dk_buf[keys, :] += lax.dot_general(ds, q[0, rows, :], tn, preferred_element_type=jnp.float32)
            dq_buf[...] += jnp.dot(ds, kw[0, keys, :], preferred_element_type=jnp.float32)

        each(back)
        dq[0, rows, :] = (dq_buf[...] * scaling).astype(jnp.bfloat16)
        return carry

    lax.fori_loop(0, TW, query_tile, 0)
    own[0, 0] = dk_buf[LAYER:2 * LAYER, :] * scaling
    own[0, 1] = dv_buf[LAYER:2 * LAYER, :]
    for side in range(2):
        part = slice(2 * side * LAYER, (2 * side + 1) * LAYER)
        edge[0, side, 0] = (dk_buf[part, :] * scaling).astype(jnp.bfloat16)
        edge[0, side, 1] = dv_buf[part, :].astype(jnp.bfloat16)
    width = 2 * TILE

    def weight_cols(at, carry):
        cols = row_block(at * width, width)
        wpart[:, cols] = lax.dot_general(
            att[...], og[:, cols], tn, preferred_element_type=jnp.float32).astype(wpart.dtype)
        return carry

    lax.fori_loop(0, og.shape[1] // width, weight_cols, 0)


def attend(allow, q, kw, vw, g, og, heads):
    def per_head(*dims):
        return pl.BlockSpec((1,) + dims, lambda h, allow: (h,) + (0,) * len(dims))

    dout = og.shape[1]
    grid_spec = pltpu.PrefetchScalarGridSpec(
        num_scalar_prefetch=1,
        grid=(heads,),
        in_specs=[per_head(LAYER, HD), per_head(3 * LAYER, HD), per_head(3 * LAYER, HD),
                  per_head(LAYER, HD), pl.BlockSpec((LAYER, dout), lambda h, allow: (0, 0))],
        out_specs=[per_head(LAYER, HD), per_head(2, LAYER, HD), per_head(2, 2, LAYER, HD),
                   pl.BlockSpec((HD, dout), lambda h, allow: (h, 0))],
        scratch_shapes=[
            pltpu.VMEM((SLOTS, TILE, TILE), jnp.float32),
            pltpu.VMEM((SLOTS, TILE, TILE), jnp.bfloat16),
            pltpu.VMEM((TILE, HD), jnp.float32),
            pltpu.VMEM((TILE, HD), jnp.float32),
            pltpu.VMEM((TILE, HD), jnp.float32),
            pltpu.VMEM((TILE, HD), jnp.float32),
            pltpu.VMEM((3 * LAYER, HD), jnp.float32),
            pltpu.VMEM((3 * LAYER, HD), jnp.float32),
            pltpu.VMEM((LAYER, HD), jnp.bfloat16),
        ])
    return pl.pallas_call(
        attend_kernel,
        out_shape=(jax.ShapeDtypeStruct((heads, LAYER, HD), jnp.bfloat16),
                   jax.ShapeDtypeStruct((heads, 2, LAYER, HD), jnp.float32),
                   jax.ShapeDtypeStruct((heads, 2, 2, LAYER, HD), jnp.bfloat16),
                   jax.ShapeDtypeStruct((heads * HD, dout), jnp.bfloat16)),
        grid_spec=grid_spec,
        compiler_params=pltpu.CompilerParams(vmem_limit_bytes=VMEM_LIMIT),
        name="attend",
    )(allow, q, kw, vw, g, og)


def out_kernel(n_uly, n_ctx, heads, dqh, own, edge, dq, dk, dv,
               inbox, low, own_sem, send_sem, recv_sem, halo_send, halo_recv):
    uly_at, ctx_at = lax.axis_index("uly"), lax.axis_index("ctx")
    rows = dq.shape[0]
    greet(n_uly, n_ctx, uly_at, ctx_at)

    def source(h, i):
        return dqh.at[h] if i == 2 else low.at[h, i]

    targets = (dk, dv, dq)

    def piece(h, i, step, owner):
        peer = lax.rem(uly_at + step, n_uly)
        return pltpu.make_async_remote_copy(
            src_ref=source(h, i).at[row_block(peer * rows, rows)],
            dst_ref=targets[i].at[:, head_cols(owner * heads + h)],
            send_sem=send_sem.at[h, i, step - 1],
            recv_sem=recv_sem.at[h, i, step - 1],
            device_id={"uly": peer}, device_id_type=MESH)

    def own_piece(h, i):
        return pltpu.make_async_copy(
            source(h, i).at[row_block(uly_at * rows, rows)],
            targets[i].at[:, head_cols(uly_at * heads + h)], own_sem.at[h, i])

    def halo(h, side):
        return pltpu.make_async_remote_copy(
            src_ref=edge.at[h, side],
            dst_ref=inbox.at[h, 1 - side],
            send_sem=halo_send.at[h, side],
            recv_sem=halo_recv.at[h, side],
            device_id={"ctx": ctx_at - 1 if side == 0 else ctx_at + 1}, device_id_type=MESH)

    def send_out(h, i):
        for step in range(1, n_uly):
            piece(h, i, step, uly_at).start()
        own_piece(h, i).start()

    for h in range(heads):
        @pl.when(ctx_at > 0)
        def _():
            halo(h, 0).start()

        @pl.when(ctx_at < n_ctx - 1)
        def _():
            halo(h, 1).start()

    for h in range(heads):
        send_out(h, 2)
    for h in range(heads):
        @pl.when(ctx_at == 0)
        def _():
            halo(h, 0).wait_recv()
            low[h] = (own[h] + inbox[h, 1].astype(jnp.float32)).astype(jnp.bfloat16)

        @pl.when(ctx_at == n_ctx - 1)
        def _():
            halo(h, 1).wait_recv()
            low[h] = (own[h] + inbox[h, 0].astype(jnp.float32)).astype(jnp.bfloat16)

        @pl.when(jnp.logical_and(ctx_at > 0, ctx_at < n_ctx - 1))
        def _():
            halo(h, 0).wait_recv()
            halo(h, 1).wait_recv()
            both = inbox[h, 0].astype(jnp.float32) + inbox[h, 1].astype(jnp.float32)
            low[h] = (own[h] + both).astype(jnp.bfloat16)

        for i in range(2):
            send_out(h, i)
    for h in range(heads):
        for i in range(3):
            for step in range(1, n_uly):
                owner = lax.rem(uly_at + n_uly - step, n_uly)
                piece(h, i, step, owner).wait_recv()
                piece(h, i, step, uly_at).wait_send()
            own_piece(h, i).wait()

        @pl.when(ctx_at > 0)
        def _():
            halo(h, 0).wait_send()

        @pl.when(ctx_at < n_ctx - 1)
        def _():
            halo(h, 1).wait_send()


def scatter_tokens(dqh, own, edge, rows, n_uly, n_ctx, heads):
    anywhere = pl.BlockSpec(memory_space=pl.ANY)
    shape = jax.ShapeDtypeStruct((rows, n_uly * heads * HD), jnp.bfloat16)
    return pl.pallas_call(
        functools.partial(out_kernel, n_uly, n_ctx, heads),
        out_shape=(shape,) * 3,
        in_specs=[anywhere, pl.BlockSpec(memory_space=pltpu.VMEM), anywhere],
        out_specs=(anywhere,) * 3,
        scratch_shapes=[
            pltpu.VMEM((heads, 2, 2, LAYER, HD), jnp.bfloat16),
            pltpu.VMEM((heads, 2, LAYER, HD), jnp.bfloat16),
            pltpu.SemaphoreType.DMA((heads, 3)),
            pltpu.SemaphoreType.DMA((heads, 3, n_uly - 1)),
            pltpu.SemaphoreType.DMA((heads, 3, n_uly - 1)),
            pltpu.SemaphoreType.DMA((heads, 2)),
            pltpu.SemaphoreType.DMA((heads, 2)),
        ],
        compiler_params=pltpu.CompilerParams(
            collective_id=1, has_side_effects=True, vmem_limit_bytes=VMEM_LIMIT),
        cost_estimate=pl.CostEstimate(flops=10 ** 10, bytes_accessed=10 ** 8, transcendentals=0),
        name="scatter_tokens",
    )(dqh, own, edge)


def allowed_tiles(tile_lists, windows, heads):
    ctx_at, uly_at = lax.axis_index("ctx"), lax.axis_index("uly")
    listed = lax.dynamic_slice_in_dim(tile_lists, ctx_at * TW, TW, 0) >= 0
    reach = lax.dynamic_slice_in_dim(windows, uly_at * heads, heads, 0)
    slot_ids = jnp.arange(SLOTS, dtype=jnp.int32)
    spot_ids = jnp.arange(TW, dtype=jnp.int32)
    near_time = jnp.abs(slot_ids // TW - 1)[None, :] <= reach[:, 0:1]
    far = jnp.abs(slot_ids[None, :] % TW - spot_ids[:, None])
    near_space = far[None] <= reach[:, 1][:, None, None]
    allowed = listed[None] & near_time[:, None, :] & near_space
    return allowed.astype(jnp.int32).reshape(-1)


def on_device(queries, key_rows, value_rows, out_grad, out_weight, tile_lists, windows):
    n_uly, n_ctx = lax.axis_size("uly"), lax.axis_size("ctx")
    heads = HEADS // n_uly
    rows = queries.shape[1]
    qh, kw, vw, g = gather_heads(
        queries[0], key_rows[0], value_rows[0], out_grad[0], out_weight, n_uly, n_ctx, heads)
    allow = allowed_tiles(tile_lists, windows, heads)
    dqh, own, edge, wpart = attend(allow, qh, kw, vw, g, out_grad[0], heads)
    total = lax.psum(wpart, ("dp", "ctx"))
    weight_grad = (total.astype(jnp.float32) / lax.axis_size("dp")).astype(jnp.bfloat16)
    dq, dk, dv = scatter_tokens(dqh, own, edge, rows, n_uly, n_ctx, heads)
    return (dq[None], dk[None], dv[None], weight_grad)


def solution(mesh):
    tokens = P("dp", ("ctx", "uly"), None)
    in_specs = (tokens, tokens, tokens, P("dp", "ctx", None), P("uly", None), P(), P())
    out_specs = (tokens, tokens, tokens, P("uly", None))
    return jax.shard_map(
        on_device, mesh=mesh, in_specs=in_specs, out_specs=out_specs, check_vma=False
    )
```

```python
import functools

import jax
import jax.numpy as jnp
from jax import lax
from jax.experimental import pallas as pl
from jax.experimental.pallas import tpu as pltpu
from jax.sharding import PartitionSpec as P

HEADS = 12
HD = 128
TILE = 384
TW = 2
SLOTS = 3 * TW
LAYER = TW * TILE
MESH = pl.DeviceIdType.MESH
LOG2E = 1.4426950408889634
VMEM_LIMIT = 56 * 1024 * 1024


def head_cols(at):
    return pl.ds(pl.multiple_of(at * HD, HD), HD)


def row_block(start, rows):
    return pl.ds(pl.multiple_of(start, rows), rows)


def greet(n_uly, n_ctx, uly_at, ctx_at):
    barrier = pltpu.get_barrier_semaphore()
    for step in range(1, n_uly):
        peer = lax.rem(uly_at + step, n_uly)
        pl.semaphore_signal(barrier, inc=1, device_id={"uly": peer}, device_id_type=MESH)

    @pl.when(ctx_at > 0)
    def _():
        pl.semaphore_signal(barrier, inc=1, device_id={"ctx": ctx_at - 1}, device_id_type=MESH)

    @pl.when(ctx_at < n_ctx - 1)
    def _():
        pl.semaphore_signal(barrier, inc=1, device_id={"ctx": ctx_at + 1}, device_id_type=MESH)

    interior = jnp.logical_and(ctx_at > 0, ctx_at < n_ctx - 1)
    pl.semaphore_wait(barrier, n_uly + interior.astype(jnp.int32))


def greet_groups(sizes):
    barrier = pltpu.get_barrier_semaphore()
    for axis, count in sizes:
        at = lax.axis_index(axis)
        for step in range(1, count):
            pl.semaphore_signal(barrier, inc=1, device_id={axis: lax.rem(at + step, count)},
                                device_id_type=MESH)
    pl.semaphore_wait(barrier, sum(count - 1 for _, count in sizes))


def in_kernel(n_uly, n_ctx, heads, q, k, v, og, ow, qh, kw, vw, g,
              og_v, ow_v, load_sem, own_sem, send_sem, recv_sem, halo_send, halo_recv):
    uly_at, ctx_at = lax.axis_index("uly"), lax.axis_index("ctx")
    rows = q.shape[0]
    loads = [pltpu.make_async_copy(og, og_v, load_sem.at[0]),
             pltpu.make_async_copy(ow, ow_v, load_sem.at[1])]
    for load in loads:
        load.start()
    triples = ((k, kw, LAYER), (v, vw, LAYER), (q, qh, 0))
    own = {}
    for h in range(heads):
        for i, (src, dst, base) in enumerate(triples):
            own[h, i] = pltpu.make_async_copy(
                src.at[:, head_cols(uly_at * heads + h)],
                dst.at[h, row_block(base + uly_at * rows, rows)],
                own_sem.at[h, i])
            own[h, i].start()
    greet(n_uly, n_ctx, uly_at, ctx_at)

    def piece(h, i, step, owner):
        src, dst, base = triples[i]
        peer = lax.rem(uly_at + step, n_uly)
        return pltpu.make_async_remote_copy(
            src_ref=src.at[:, head_cols(peer * heads + h)],
            dst_ref=dst.at[h, row_block(base + owner * rows, rows)],
            send_sem=send_sem.at[h, i, step - 1],
            recv_sem=recv_sem.at[h, i, step - 1],
            device_id={"uly": peer}, device_id_type=MESH)

    order = [(h, i) for h in range(heads) for i in range(2)] + [(h, 2) for h in range(heads)]
    for h, i in order:
        for step in range(1, n_uly):
            piece(h, i, step, uly_at).start()

    for load in loads:
        load.wait()

    def grad_rows(at, carry):
        chunk = row_block(at * TILE, TILE)
        out = lax.dot_general(og_v[chunk, :], ow_v[...], (((1,), (1,)), ((), ())),
                              preferred_element_type=jnp.float32).astype(jnp.bfloat16)
        for h in range(heads):
            g[h, chunk, :] = out[:, h * HD:(h + 1) * HD]
        return carry

    lax.fori_loop(0, TW, grad_rows, 0)

    def arrived(h, i):
        own[h, i].wait()
        for step in range(1, n_uly):
            owner = lax.rem(uly_at + n_uly - step, n_uly)
            piece(h, i, step, owner).wait_recv()

    def halo(h, i, side):
        buf = triples[i][1]
        slot = 2 if side == 0 else 0
        return pltpu.make_async_remote_copy(
            src_ref=buf.at[h, pl.ds(LAYER, LAYER)],
            dst_ref=buf.at[h, pl.ds(slot * LAYER, LAYER)],
            send_sem=halo_send.at[h, i, side],
            recv_sem=halo_recv.at[h, i, side],
            device_id={"ctx": ctx_at - 1 if side == 0 else ctx_at + 1}, device_id_type=MESH)

    for h in range(heads):
        for i in range(2):
            arrived(h, i)

            @pl.when(ctx_at > 0)
            def _():
                halo(h, i, 0).start()

            @pl.when(ctx_at < n_ctx - 1)
            def _():
                halo(h, i, 1).start()

    for h in range(heads):
        arrived(h, 2)
    for h in range(heads):
        for i in range(2):
            @pl.when(ctx_at > 0)
            def _():
                halo(h, i, 0).wait_send()
                halo(h, i, 1).wait_recv()

            @pl.when(ctx_at < n_ctx - 1)
            def _():
                halo(h, i, 1).wait_send()
                halo(h, i, 0).wait_recv()
    for h, i in order:
        for step in range(1, n_uly):
            piece(h, i, step, uly_at).wait_send()


def gather_heads(q, k, v, og, ow, n_uly, n_ctx, heads):
    span = LAYER
    anywhere = pl.BlockSpec(memory_space=pl.ANY)
    return pl.pallas_call(
        functools.partial(in_kernel, n_uly, n_ctx, heads),
        out_shape=(jax.ShapeDtypeStruct((heads, span, HD), jnp.bfloat16),
                   jax.ShapeDtypeStruct((heads, 3 * span, HD), jnp.bfloat16),
                   jax.ShapeDtypeStruct((heads, 3 * span, HD), jnp.bfloat16),
                   jax.ShapeDtypeStruct((heads, span, HD), jnp.bfloat16)),
        in_specs=[anywhere] * 5,
        out_specs=(anywhere, anywhere, anywhere, pl.BlockSpec(memory_space=pltpu.VMEM)),
        scratch_shapes=[
            pltpu.VMEM(og.shape, jnp.bfloat16),
            pltpu.VMEM(ow.shape, jnp.bfloat16),
            pltpu.SemaphoreType.DMA((2,)),
            pltpu.SemaphoreType.DMA((heads, 3)),
            pltpu.SemaphoreType.DMA((heads, 3, n_uly - 1)),
            pltpu.SemaphoreType.DMA((heads, 3, n_uly - 1)),
            pltpu.SemaphoreType.DMA((heads, 2, 2)),
            pltpu.SemaphoreType.DMA((heads, 2, 2)),
        ],
        compiler_params=pltpu.CompilerParams(
            collective_id=0, has_side_effects=True, vmem_limit_bytes=VMEM_LIMIT),
        name="gather_heads",
    )(q, k, v, og, ow)


def lane_fold(x, op):
    out = x[:, 0:HD]
    for at in range(HD, x.shape[1], HD):
        out = op(out, x[:, at:at + HD])
    return out


def attend_kernel(allow, q, kw, vw, g, og, dq, own, edge, wpart,
                  s_buf, p_buf, m_buf, l_buf, o_buf, dq_buf, dk_buf, dv_buf, att):
    head = pl.program_id(0)
    scaling = HD ** (-0.5)
    dk_buf[...] = jnp.zeros_like(dk_buf)
    dv_buf[...] = jnp.zeros_like(dv_buf)
    nt = (((1,), (1,)), ((), ()))
    tn = (((0,), (0,)), ((), ()))

    def query_tile(spot, carry):
        rows = row_block(spot * TILE, TILE)
        flags = (head * TW + spot) * SLOTS

        def each(body):
            def step(slot, c):
                @pl.when(allow[flags + slot] > 0)
                def _():
                    body(slot, row_block(slot * TILE, TILE))
                return c
            lax.fori_loop(0, SLOTS, step, 0)

        m_buf[...] = jnp.full_like(m_buf, -jnp.inf)
        l_buf[...] = jnp.zeros_like(l_buf)
        o_buf[...] = jnp.zeros_like(o_buf)
        dq_buf[...] = jnp.zeros_like(dq_buf)

        def score(slot, keys):
            s = lax.dot_general(q[0, rows, :], kw[0, keys, :], nt, preferred_element_type=jnp.float32)
            s_buf[slot] = s
            m_buf[...] = jnp.maximum(m_buf[...], lane_fold(s, jnp.maximum))

        each(score)
        top = jnp.max(m_buf[...], axis=1, keepdims=True)

        def weigh(slot, keys):
            p = jnp.exp2((s_buf[slot] - top) * (scaling * LOG2E))
            l_buf[...] += lane_fold(p, jnp.add)
            low = p.astype(jnp.bfloat16)
            p_buf[slot] = low
            o_buf[...] += jnp.dot(low, vw[0, keys, :], preferred_element_type=jnp.float32)

        each(weigh)
        inv = 1.0 / jnp.sum(l_buf[...], axis=1, keepdims=True)
        out = o_buf[...] * inv
        att[rows, :] = out.astype(jnp.bfloat16)
        gp = (g[0, rows, :].astype(jnp.float32) * inv).astype(jnp.bfloat16)
        delta = jnp.sum(out * gp.astype(jnp.float32), axis=1, keepdims=True)

        def back(slot, keys):
            low = p_buf[slot]
            dp = lax.dot_general(gp, vw[0, keys, :], nt, preferred_element_type=jnp.float32)
            ds = (low.astype(jnp.float32) * (dp - delta)).astype(jnp.bfloat16)
            dv_buf[keys, :] += lax.dot_general(low, gp, tn, preferred_element_type=jnp.float32)
            dk_buf[keys, :] += lax.dot_general(ds, q[0, rows, :], tn, preferred_element_type=jnp.float32)
            dq_buf[...] += jnp.dot(ds, kw[0, keys, :], preferred_element_type=jnp.float32)

        each(back)
        dq[0, rows, :] = (dq_buf[...] * scaling).astype(jnp.bfloat16)
        return carry

    lax.fori_loop(0, TW, query_tile, 0)
    own[0, 0] = dk_buf[LAYER:2 * LAYER, :] * scaling
    own[0, 1] = dv_buf[LAYER:2 * LAYER, :]
    for side in range(2):
        part = slice(2 * side * LAYER, (2 * side + 1) * LAYER)
        edge[0, side, 0] = (dk_buf[part, :] * scaling).astype(jnp.bfloat16)
        edge[0, side, 1] = dv_buf[part, :].astype(jnp.bfloat16)
    width = 2 * TILE

    def weight_cols(at, carry):
        cols = row_block(at * width, width)
        wpart[:, cols] = lax.dot_general(
            att[...], og[:, cols], tn, preferred_element_type=jnp.float32).astype(wpart.dtype)
        return carry

    lax.fori_loop(0, og.shape[1] // width, weight_cols, 0)


def attend(allow, q, kw, vw, g, og, heads):
    def per_head(*dims):
        return pl.BlockSpec((1,) + dims, lambda h, allow: (h,) + (0,) * len(dims))

    dout = og.shape[1]
    grid_spec = pltpu.PrefetchScalarGridSpec(
        num_scalar_prefetch=1,
        grid=(heads,),
        in_specs=[per_head(LAYER, HD), per_head(3 * LAYER, HD), per_head(3 * LAYER, HD),
                  per_head(LAYER, HD), pl.BlockSpec((LAYER, dout), lambda h, allow: (0, 0))],
        out_specs=[per_head(LAYER, HD), per_head(2, LAYER, HD), per_head(2, 2, LAYER, HD),
                   pl.BlockSpec((HD, dout), lambda h, allow: (h, 0))],
        scratch_shapes=[
            pltpu.VMEM((SLOTS, TILE, TILE), jnp.float32),
            pltpu.VMEM((SLOTS, TILE, TILE), jnp.bfloat16),
            pltpu.VMEM((TILE, HD), jnp.float32),
            pltpu.VMEM((TILE, HD), jnp.float32),
            pltpu.VMEM((TILE, HD), jnp.float32),
            pltpu.VMEM((TILE, HD), jnp.float32),
            pltpu.VMEM((3 * LAYER, HD), jnp.float32),
            pltpu.VMEM((3 * LAYER, HD), jnp.float32),
            pltpu.VMEM((LAYER, HD), jnp.bfloat16),
        ])
    return pl.pallas_call(
        attend_kernel,
        out_shape=(jax.ShapeDtypeStruct((heads, LAYER, HD), jnp.bfloat16),
                   jax.ShapeDtypeStruct((heads, 2, LAYER, HD), jnp.float32),
                   jax.ShapeDtypeStruct((heads, 2, 2, LAYER, HD), jnp.bfloat16),
                   jax.ShapeDtypeStruct((heads * HD, dout), jnp.bfloat16)),
        grid_spec=grid_spec,
        compiler_params=pltpu.CompilerParams(vmem_limit_bytes=VMEM_LIMIT),
        name="attend",
    )(allow, q, kw, vw, g, og)


def chunk_of(n_dp, dout):
    bands = 1 if (dout // n_dp) % 128 == 0 else 2
    return bands, HD // 4 // bands, dout * bands // n_dp


class WeightSum:
    def __init__(self, n_dp, part, out, in1, sum1, in2, sum2, in3, final, sems, dp_sems, own_sem):
        self.n_dp, self.part, self.out = n_dp, part, out
        self.in1, self.sum1, self.in2, self.sum2, self.in3, self.final = in1, sum1, in2, sum2, in3, final
        self.sems, self.dp_sems, self.own_sem = sems, dp_sems, own_sem
        ctx_at = lax.axis_index("ctx")
        self.dp_at = lax.axis_index("dp")
        self.core, self.far = lax.rem(ctx_at, 2), ctx_at // 2
        self.core_peer = ctx_at + 1 - 2 * self.core
        self.far_peer = lax.rem(ctx_at + 2, 4)
        self.bands, self.height, self.width = chunk_of(n_dp, part.shape[1])

    def cols(self, at):
        return pl.ds(pl.multiple_of((at // self.bands) * self.width, self.width), self.width)

    def band(self, at):
        return row_block(lax.rem(at, self.bands) * self.height, self.height)

    def chunk_rows(self, h, at):
        start = h * HD + self.core * (HD // 2) + self.far * (HD // 4)
        return row_block(start + lax.rem(at, self.bands) * self.height, self.height)

    def copy(self, kind, h, src, dst, peer):
        return pltpu.make_async_remote_copy(
            src_ref=src, dst_ref=dst, send_sem=self.sems.at[0, kind, h],
            recv_sem=self.sems.at[1, kind, h], device_id={"ctx": peer}, device_id_type=MESH)

    def dp_copy(self, kind, h, step, src, dst):
        return pltpu.make_async_remote_copy(
            src_ref=src, dst_ref=dst, send_sem=self.dp_sems.at[0, kind, h, step - 1],
            recv_sem=self.dp_sems.at[1, kind, h, step - 1],
            device_id={"dp": lax.rem(self.dp_at + step, self.n_dp)}, device_id_type=MESH)

    def core_rows(self, h, core):
        return row_block(h * HD + core * (HD // 2), HD // 2)

    def far_rows(self, h, far):
        return row_block(h * HD + self.core * (HD // 2) + far * (HD // 4), HD // 4)

    def reduce1(self, h):
        return self.copy(0, h, self.part.at[self.core_rows(h, 1 - self.core)], self.in1.at[h],
                         self.core_peer)

    def reduce2(self, h):
        return self.copy(1, h, self.sum1.at[h, row_block((1 - self.far) * (HD // 4), HD // 4)],
                         self.in2.at[h], self.far_peer)

    def reduce3(self, h, step):
        peer = lax.rem(self.dp_at + step, self.n_dp)
        return self.dp_copy(0, h, step, self.sum2.at[h, self.band(peer), self.cols(peer)],
                            self.in3.at[h, step - 1])

    def share1(self, h, step, owner):
        return self.dp_copy(1, h, step, self.final.at[h],
                            self.out.at[self.chunk_rows(h, owner), self.cols(owner)])

    def own_copy(self, h):
        return pltpu.make_async_copy(
            self.final.at[h], self.out.at[self.chunk_rows(h, self.dp_at), self.cols(self.dp_at)],
            self.own_sem.at[h])

    def share2(self, h, far):
        rows = self.far_rows(h, far)
        return self.copy(2, h, self.out.at[rows], self.out.at[rows], self.far_peer)

    def share3(self, h, core):
        rows = self.core_rows(h, core)
        return self.copy(3, h, self.out.at[rows], self.out.at[rows], self.core_peer)

    def step0(self, h):
        self.reduce1(h).start()

    def step1(self, h):
        self.reduce1(h).wait_recv()
        mine = self.part[self.core_rows(h, self.core), :].astype(jnp.float32)
        self.sum1[h] = (mine + self.in1[h].astype(jnp.float32)).astype(jnp.bfloat16)
        self.reduce2(h).start()

    def step2(self, h):
        self.reduce2(h).wait_recv()
        mine = self.sum1[h, row_block(self.far * (HD // 4), HD // 4), :].astype(jnp.float32)
        self.sum2[h] = (mine + self.in2[h].astype(jnp.float32)).astype(jnp.bfloat16)
        for step in range(1, self.n_dp):
            self.reduce3(h, step).start()

    def step3(self, h):
        total = self.sum2[h, self.band(self.dp_at), self.cols(self.dp_at)].astype(jnp.float32)
        for step in range(1, self.n_dp):
            self.reduce3(h, step).wait_recv()
            total = total + self.in3[h, step - 1].astype(jnp.float32)
        self.final[h] = (total / self.n_dp).astype(jnp.bfloat16)
        self.own_copy(h).start()
        for step in range(1, self.n_dp):
            self.share1(h, step, self.dp_at).start()

    def step4(self, h):
        self.own_copy(h).wait()
        for step in range(1, self.n_dp):
            self.share1(h, step, lax.rem(self.dp_at + self.n_dp - step, self.n_dp)).wait_recv()
        self.share2(h, self.far).start()

    def step5(self, h):
        self.share2(h, 1 - self.far).wait_recv()
        self.share3(h, self.core).start()

    def finish(self, h):
        self.share3(h, 1 - self.core).wait_recv()
        self.share3(h, self.core).wait_send()
        self.share2(h, self.far).wait_send()
        self.reduce1(h).wait_send()
        self.reduce2(h).wait_send()
        for step in range(1, self.n_dp):
            self.reduce3(h, step).wait_send()
            self.share1(h, step, self.dp_at).wait_send()


def out_kernel(n_dp, n_uly, n_ctx, heads, dqh, own, edge, wpart, dq, dk, dv, wout,
               inbox, low, own_sem, send_sem, recv_sem, halo_send, halo_recv, *weight_refs):
    uly_at, ctx_at = lax.axis_index("uly"), lax.axis_index("ctx")
    rows = dq.shape[0]
    weight = WeightSum(n_dp, wpart, wout, *weight_refs)
    greet_groups((("uly", n_uly), ("ctx", n_ctx), ("dp", n_dp)))

    def source(h, i):
        return dqh.at[h] if i == 2 else low.at[h, i]

    targets = (dk, dv, dq)

    def piece(h, i, step, owner):
        peer = lax.rem(uly_at + step, n_uly)
        return pltpu.make_async_remote_copy(
            src_ref=source(h, i).at[row_block(peer * rows, rows)],
            dst_ref=targets[i].at[:, head_cols(owner * heads + h)],
            send_sem=send_sem.at[h, i, step - 1],
            recv_sem=recv_sem.at[h, i, step - 1],
            device_id={"uly": peer}, device_id_type=MESH)

    def own_piece(h, i):
        return pltpu.make_async_copy(
            source(h, i).at[row_block(uly_at * rows, rows)],
            targets[i].at[:, head_cols(uly_at * heads + h)], own_sem.at[h, i])

    def halo(h, side):
        return pltpu.make_async_remote_copy(
            src_ref=edge.at[h, side],
            dst_ref=inbox.at[h, 1 - side],
            send_sem=halo_send.at[h, side],
            recv_sem=halo_recv.at[h, side],
            device_id={"ctx": ctx_at - 1 if side == 0 else ctx_at + 1}, device_id_type=MESH)

    def send_out(h, i):
        for step in range(1, n_uly):
            piece(h, i, step, uly_at).start()
        own_piece(h, i).start()

    for h in range(heads):
        @pl.when(ctx_at > 0)
        def _():
            halo(h, 0).start()

        @pl.when(ctx_at < n_ctx - 1)
        def _():
            halo(h, 1).start()

    for h in range(heads):
        weight.step0(h)
    for h in range(heads):
        send_out(h, 2)
    for h in range(heads):
        weight.step1(h)
    for h in range(heads):
        @pl.when(ctx_at == 0)
        def _():
            halo(h, 0).wait_recv()
            low[h] = (own[h] + inbox[h, 1].astype(jnp.float32)).astype(jnp.bfloat16)

        @pl.when(ctx_at == n_ctx - 1)
        def _():
            halo(h, 1).wait_recv()
            low[h] = (own[h] + inbox[h, 0].astype(jnp.float32)).astype(jnp.bfloat16)

        @pl.when(jnp.logical_and(ctx_at > 0, ctx_at < n_ctx - 1))
        def _():
            halo(h, 0).wait_recv()
            halo(h, 1).wait_recv()
            both = inbox[h, 0].astype(jnp.float32) + inbox[h, 1].astype(jnp.float32)
            low[h] = (own[h] + both).astype(jnp.bfloat16)

        for i in range(2):
            send_out(h, i)
    stages = (weight.step2, weight.step3, weight.step4, weight.step5)
    for at in range(heads + len(stages) - 1):
        for lag, stage in enumerate(stages):
            if 0 <= at - lag < heads:
                stage(at - lag)
    for h in range(heads):
        weight.finish(h)
    for h in range(heads):
        for i in range(3):
            for step in range(1, n_uly):
                owner = lax.rem(uly_at + n_uly - step, n_uly)
                piece(h, i, step, owner).wait_recv()
                piece(h, i, step, uly_at).wait_send()
            own_piece(h, i).wait()

        @pl.when(ctx_at > 0)
        def _():
            halo(h, 0).wait_send()

        @pl.when(ctx_at < n_ctx - 1)
        def _():
            halo(h, 1).wait_send()


def scatter_tokens(dqh, own, edge, wpart, rows, n_dp, n_uly, n_ctx, heads):
    anywhere = pl.BlockSpec(memory_space=pl.ANY)
    dout = wpart.shape[1]
    _, height, width = chunk_of(n_dp, dout)
    shape = jax.ShapeDtypeStruct((rows, n_uly * heads * HD), jnp.bfloat16)
    return pl.pallas_call(
        functools.partial(out_kernel, n_dp, n_uly, n_ctx, heads),
        out_shape=(shape,) * 3 + (jax.ShapeDtypeStruct(wpart.shape, jnp.bfloat16),),
        in_specs=[anywhere, pl.BlockSpec(memory_space=pltpu.VMEM), anywhere,
                  pl.BlockSpec(memory_space=pltpu.VMEM)],
        out_specs=(anywhere,) * 4,
        scratch_shapes=[
            pltpu.VMEM((heads, 2, 2, LAYER, HD), jnp.bfloat16),
            pltpu.VMEM((heads, 2, LAYER, HD), jnp.bfloat16),
            pltpu.SemaphoreType.DMA((heads, 3)),
            pltpu.SemaphoreType.DMA((heads, 3, n_uly - 1)),
            pltpu.SemaphoreType.DMA((heads, 3, n_uly - 1)),
            pltpu.SemaphoreType.DMA((heads, 2)),
            pltpu.SemaphoreType.DMA((heads, 2)),
            pltpu.VMEM((heads, HD // 2, dout), jnp.bfloat16),
            pltpu.VMEM((heads, HD // 2, dout), jnp.bfloat16),
            pltpu.VMEM((heads, HD // 4, dout), jnp.bfloat16),
            pltpu.VMEM((heads, HD // 4, dout), jnp.bfloat16),
            pltpu.VMEM((heads, n_dp - 1, height, width), jnp.bfloat16),
            pltpu.VMEM((heads, height, width), jnp.bfloat16),
            pltpu.SemaphoreType.DMA((2, 4, heads)),
            pltpu.SemaphoreType.DMA((2, 2, heads, n_dp - 1)),
            pltpu.SemaphoreType.DMA((heads,)),
        ],
        compiler_params=pltpu.CompilerParams(
            collective_id=1, has_side_effects=True, vmem_limit_bytes=VMEM_LIMIT),
        name="scatter_tokens",
    )(dqh, own, edge, wpart)


def allowed_tiles(tile_lists, windows, heads):
    ctx_at, uly_at = lax.axis_index("ctx"), lax.axis_index("uly")
    listed = lax.dynamic_slice_in_dim(tile_lists, ctx_at * TW, TW, 0) >= 0
    reach = lax.dynamic_slice_in_dim(windows, uly_at * heads, heads, 0)
    slot_ids = jnp.arange(SLOTS, dtype=jnp.int32)
    spot_ids = jnp.arange(TW, dtype=jnp.int32)
    near_time = jnp.abs(slot_ids // TW - 1)[None, :] <= reach[:, 0:1]
    far = jnp.abs(slot_ids[None, :] % TW - spot_ids[:, None])
    near_space = far[None] <= reach[:, 1][:, None, None]
    allowed = listed[None] & near_time[:, None, :] & near_space
    return allowed.astype(jnp.int32).reshape(-1)


def on_device(queries, key_rows, value_rows, out_grad, out_weight, tile_lists, windows):
    n_uly, n_ctx = lax.axis_size("uly"), lax.axis_size("ctx")
    heads = HEADS // n_uly
    rows = queries.shape[1]
    qh, kw, vw, g = gather_heads(
        queries[0], key_rows[0], value_rows[0], out_grad[0], out_weight, n_uly, n_ctx, heads)
    allow = allowed_tiles(tile_lists, windows, heads)
    dqh, own, edge, wpart = attend(allow, qh, kw, vw, g, out_grad[0], heads)
    dq, dk, dv, weight_grad = scatter_tokens(
        dqh, own, edge, wpart, rows, lax.axis_size("dp"), n_uly, n_ctx, heads)
    return (dq[None], dk[None], dv[None], weight_grad)


def solution(mesh):
    tokens = P("dp", ("ctx", "uly"), None)
    in_specs = (tokens, tokens, tokens, P("dp", "ctx", None), P("uly", None), P(), P())
    out_specs = (tokens, tokens, tokens, P("uly", None))
    return jax.shard_map(
        on_device, mesh=mesh, in_specs=in_specs, out_specs=out_specs, check_vma=False
    )
```

```python
import functools

import jax
import jax.numpy as jnp
from jax import lax
from jax.experimental import pallas as pl
from jax.experimental.pallas import tpu as pltpu
from jax.sharding import PartitionSpec as P

HEADS = 12
HD = 128
TILE = 384
TW = 2
SLOTS = 3 * TW
LAYER = TW * TILE
MESH = pl.DeviceIdType.MESH
LOG2E = 1.4426950408889634
VMEM_LIMIT = 56 * 1024 * 1024


def head_cols(at):
    return pl.ds(pl.multiple_of(at * HD, HD), HD)


def row_block(start, rows):
    return pl.ds(pl.multiple_of(start, rows), rows)


def greet(n_uly, n_ctx, uly_at, ctx_at):
    barrier = pltpu.get_barrier_semaphore()
    for step in range(1, n_uly):
        peer = lax.rem(uly_at + step, n_uly)
        pl.semaphore_signal(barrier, inc=1, device_id={"uly": peer}, device_id_type=MESH)

    @pl.when(ctx_at > 0)
    def _():
        pl.semaphore_signal(barrier, inc=1, device_id={"ctx": ctx_at - 1}, device_id_type=MESH)

    @pl.when(ctx_at < n_ctx - 1)
    def _():
        pl.semaphore_signal(barrier, inc=1, device_id={"ctx": ctx_at + 1}, device_id_type=MESH)

    interior = jnp.logical_and(ctx_at > 0, ctx_at < n_ctx - 1)
    pl.semaphore_wait(barrier, n_uly + interior.astype(jnp.int32))


def greet_groups(sizes):
    barrier = pltpu.get_barrier_semaphore()
    for axis, count in sizes:
        at = lax.axis_index(axis)
        for step in range(1, count):
            pl.semaphore_signal(barrier, inc=1, device_id={axis: lax.rem(at + step, count)},
                                device_id_type=MESH)
    pl.semaphore_wait(barrier, sum(count - 1 for _, count in sizes))


def in_kernel(n_uly, n_ctx, heads, q, k, v, og, ow, qh, kw, vw, g,
              og_v, ow_v, load_sem, own_sem, send_sem, recv_sem, halo_send, halo_recv):
    uly_at, ctx_at = lax.axis_index("uly"), lax.axis_index("ctx")
    rows = q.shape[0]
    loads = [pltpu.make_async_copy(og, og_v, load_sem.at[0]),
             pltpu.make_async_copy(ow, ow_v, load_sem.at[1])]
    for load in loads:
        load.start()
    triples = ((k, kw, LAYER), (v, vw, LAYER), (q, qh, 0))
    own = {}
    for h in range(heads):
        for i, (src, dst, base) in enumerate(triples):
            own[h, i] = pltpu.make_async_copy(
                src.at[:, head_cols(uly_at * heads + h)],
                dst.at[h, row_block(base + uly_at * rows, rows)],
                own_sem.at[h, i])
            own[h, i].start()
    greet(n_uly, n_ctx, uly_at, ctx_at)

    def piece(h, i, step, owner):
        src, dst, base = triples[i]
        peer = lax.rem(uly_at + step, n_uly)
        return pltpu.make_async_remote_copy(
            src_ref=src.at[:, head_cols(peer * heads + h)],
            dst_ref=dst.at[h, row_block(base + owner * rows, rows)],
            send_sem=send_sem.at[h, i, step - 1],
            recv_sem=recv_sem.at[h, i, step - 1],
            device_id={"uly": peer}, device_id_type=MESH)

    order = [(h, i) for h in range(heads) for i in range(2)] + [(h, 2) for h in range(heads)]
    for h, i in order:
        for step in range(1, n_uly):
            piece(h, i, step, uly_at).start()

    for load in loads:
        load.wait()

    def grad_rows(at, carry):
        chunk = row_block(at * TILE, TILE)
        out = lax.dot_general(og_v[chunk, :], ow_v[...], (((1,), (1,)), ((), ())),
                              preferred_element_type=jnp.float32).astype(jnp.bfloat16)
        for h in range(heads):
            g[h, chunk, :] = out[:, h * HD:(h + 1) * HD]
        return carry

    lax.fori_loop(0, TW, grad_rows, 0)

    def arrived(h, i):
        own[h, i].wait()
        for step in range(1, n_uly):
            owner = lax.rem(uly_at + n_uly - step, n_uly)
            piece(h, i, step, owner).wait_recv()

    def halo(h, i, side):
        buf = triples[i][1]
        slot = 2 if side == 0 else 0
        return pltpu.make_async_remote_copy(
            src_ref=buf.at[h, pl.ds(LAYER, LAYER)],
            dst_ref=buf.at[h, pl.ds(slot * LAYER, LAYER)],
            send_sem=halo_send.at[h, i, side],
            recv_sem=halo_recv.at[h, i, side],
            device_id={"ctx": ctx_at - 1 if side == 0 else ctx_at + 1}, device_id_type=MESH)

    for h in range(heads):
        for i in range(2):
            arrived(h, i)

            @pl.when(ctx_at > 0)
            def _():
                halo(h, i, 0).start()

            @pl.when(ctx_at < n_ctx - 1)
            def _():
                halo(h, i, 1).start()

    for h in range(heads):
        arrived(h, 2)
    for h in range(heads):
        for i in range(2):
            @pl.when(ctx_at > 0)
            def _():
                halo(h, i, 0).wait_send()
                halo(h, i, 1).wait_recv()

            @pl.when(ctx_at < n_ctx - 1)
            def _():
                halo(h, i, 1).wait_send()
                halo(h, i, 0).wait_recv()
    for h, i in order:
        for step in range(1, n_uly):
            piece(h, i, step, uly_at).wait_send()


def gather_heads(q, k, v, og, ow, n_uly, n_ctx, heads):
    span = LAYER
    anywhere = pl.BlockSpec(memory_space=pl.ANY)
    return pl.pallas_call(
        functools.partial(in_kernel, n_uly, n_ctx, heads),
        out_shape=(jax.ShapeDtypeStruct((heads, span, HD), jnp.bfloat16),
                   jax.ShapeDtypeStruct((heads, 3 * span, HD), jnp.bfloat16),
                   jax.ShapeDtypeStruct((heads, 3 * span, HD), jnp.bfloat16),
                   jax.ShapeDtypeStruct((heads, span, HD), jnp.bfloat16)),
        in_specs=[anywhere] * 5,
        out_specs=(anywhere, anywhere, anywhere, pl.BlockSpec(memory_space=pltpu.VMEM)),
        scratch_shapes=[
            pltpu.VMEM(og.shape, jnp.bfloat16),
            pltpu.VMEM(ow.shape, jnp.bfloat16),
            pltpu.SemaphoreType.DMA((2,)),
            pltpu.SemaphoreType.DMA((heads, 3)),
            pltpu.SemaphoreType.DMA((heads, 3, n_uly - 1)),
            pltpu.SemaphoreType.DMA((heads, 3, n_uly - 1)),
            pltpu.SemaphoreType.DMA((heads, 2, 2)),
            pltpu.SemaphoreType.DMA((heads, 2, 2)),
        ],
        compiler_params=pltpu.CompilerParams(
            collective_id=0, has_side_effects=True, vmem_limit_bytes=VMEM_LIMIT),
        name="gather_heads",
    )(q, k, v, og, ow)


def lane_fold(x, op):
    out = x[:, 0:HD]
    for at in range(HD, x.shape[1], HD):
        out = op(out, x[:, at:at + HD])
    return out


def attend_kernel(allow, q, kw, vw, g, og, dq, own, edge, wpart,
                  s_buf, p_buf, m_buf, l_buf, o_buf, dq_buf, dk_buf, dv_buf, att):
    head = pl.program_id(0)
    scaling = HD ** (-0.5)
    dk_buf[...] = jnp.zeros_like(dk_buf)
    dv_buf[...] = jnp.zeros_like(dv_buf)
    nt = (((1,), (1,)), ((), ()))
    tn = (((0,), (0,)), ((), ()))

    def query_tile(spot, carry):
        rows = row_block(spot * TILE, TILE)
        flags = (head * TW + spot) * SLOTS

        def each(body):
            def step(slot, c):
                @pl.when(allow[flags + slot] > 0)
                def _():
                    body(slot, row_block(slot * TILE, TILE))
                return c
            lax.fori_loop(0, SLOTS, step, 0)

        m_buf[...] = jnp.full_like(m_buf, -jnp.inf)
        l_buf[...] = jnp.zeros_like(l_buf)
        o_buf[...] = jnp.zeros_like(o_buf)
        dq_buf[...] = jnp.zeros_like(dq_buf)

        def score(slot, keys):
            s = lax.dot_general(q[0, rows, :], kw[0, keys, :], nt, preferred_element_type=jnp.float32)
            s_buf[slot] = s
            m_buf[...] = jnp.maximum(m_buf[...], lane_fold(s, jnp.maximum))

        each(score)
        top = jnp.max(m_buf[...], axis=1, keepdims=True)

        def weigh(slot, keys):
            p = jnp.exp2((s_buf[slot] - top) * (scaling * LOG2E))
            l_buf[...] += lane_fold(p, jnp.add)
            low = p.astype(jnp.bfloat16)
            p_buf[slot] = low
            o_buf[...] += jnp.dot(low, vw[0, keys, :], preferred_element_type=jnp.float32)

        each(weigh)
        inv = 1.0 / jnp.sum(l_buf[...], axis=1, keepdims=True)
        out = o_buf[...] * inv
        att[rows, :] = out.astype(jnp.bfloat16)
        gp = (g[0, rows, :].astype(jnp.float32) * inv).astype(jnp.bfloat16)
        delta = jnp.sum(out * gp.astype(jnp.float32), axis=1, keepdims=True)

        def back(slot, keys):
            low = p_buf[slot]
            dp = lax.dot_general(gp, vw[0, keys, :], nt, preferred_element_type=jnp.float32)
            ds = low * (dp - delta).astype(jnp.bfloat16)
            dv_buf[keys, :] += lax.dot_general(low, gp, tn, preferred_element_type=jnp.float32)
            dk_buf[keys, :] += lax.dot_general(ds, q[0, rows, :], tn, preferred_element_type=jnp.float32)
            dq_buf[...] += jnp.dot(ds, kw[0, keys, :], preferred_element_type=jnp.float32)

        each(back)
        dq[0, rows, :] = (dq_buf[...] * scaling).astype(jnp.bfloat16)
        return carry

    lax.fori_loop(0, TW, query_tile, 0)
    own[0, 0] = dk_buf[LAYER:2 * LAYER, :] * scaling
    own[0, 1] = dv_buf[LAYER:2 * LAYER, :]
    for side in range(2):
        part = slice(2 * side * LAYER, (2 * side + 1) * LAYER)
        edge[0, side, 0] = (dk_buf[part, :] * scaling).astype(jnp.bfloat16)
        edge[0, side, 1] = dv_buf[part, :].astype(jnp.bfloat16)
    width = 2 * TILE

    def weight_cols(at, carry):
        cols = row_block(at * width, width)
        wpart[:, cols] = lax.dot_general(
            att[...], og[:, cols], tn, preferred_element_type=jnp.float32).astype(wpart.dtype)
        return carry

    lax.fori_loop(0, og.shape[1] // width, weight_cols, 0)


def attend(allow, q, kw, vw, g, og, heads):
    def per_head(*dims):
        return pl.BlockSpec((1,) + dims, lambda h, allow: (h,) + (0,) * len(dims))

    dout = og.shape[1]
    grid_spec = pltpu.PrefetchScalarGridSpec(
        num_scalar_prefetch=1,
        grid=(heads,),
        in_specs=[per_head(LAYER, HD), per_head(3 * LAYER, HD), per_head(3 * LAYER, HD),
                  per_head(LAYER, HD), pl.BlockSpec((LAYER, dout), lambda h, allow: (0, 0))],
        out_specs=[per_head(LAYER, HD), per_head(2, LAYER, HD), per_head(2, 2, LAYER, HD),
                   pl.BlockSpec((HD, dout), lambda h, allow: (h, 0))],
        scratch_shapes=[
            pltpu.VMEM((SLOTS, TILE, TILE), jnp.float32),
            pltpu.VMEM((SLOTS, TILE, TILE), jnp.bfloat16),
            pltpu.VMEM((TILE, HD), jnp.float32),
            pltpu.VMEM((TILE, HD), jnp.float32),
            pltpu.VMEM((TILE, HD), jnp.float32),
            pltpu.VMEM((TILE, HD), jnp.float32),
            pltpu.VMEM((3 * LAYER, HD), jnp.float32),
            pltpu.VMEM((3 * LAYER, HD), jnp.float32),
            pltpu.VMEM((LAYER, HD), jnp.bfloat16),
        ])
    return pl.pallas_call(
        attend_kernel,
        out_shape=(jax.ShapeDtypeStruct((heads, LAYER, HD), jnp.bfloat16),
                   jax.ShapeDtypeStruct((heads, 2, LAYER, HD), jnp.float32),
                   jax.ShapeDtypeStruct((heads, 2, 2, LAYER, HD), jnp.bfloat16),
                   jax.ShapeDtypeStruct((heads * HD, dout), jnp.bfloat16)),
        grid_spec=grid_spec,
        compiler_params=pltpu.CompilerParams(vmem_limit_bytes=VMEM_LIMIT),
        name="attend",
    )(allow, q, kw, vw, g, og)


def chunk_of(n_dp, dout):
    bands = 1 if (dout // n_dp) % 128 == 0 else 2
    return bands, HD // 4 // bands, dout * bands // n_dp


class WeightSum:
    def __init__(self, n_dp, part, out, in1, sum1, in2, sum2, in3, final, sems, dp_sems, own_sem):
        self.n_dp, self.part, self.out = n_dp, part, out
        self.in1, self.sum1, self.in2, self.sum2, self.in3, self.final = in1, sum1, in2, sum2, in3, final
        self.sems, self.dp_sems, self.own_sem = sems, dp_sems, own_sem
        ctx_at = lax.axis_index("ctx")
        self.dp_at = lax.axis_index("dp")
        self.core, self.far = lax.rem(ctx_at, 2), ctx_at // 2
        self.core_peer = ctx_at + 1 - 2 * self.core
        self.far_peer = lax.rem(ctx_at + 2, 4)
        self.bands, self.height, self.width = chunk_of(n_dp, part.shape[1])

    def cols(self, at):
        return pl.ds(pl.multiple_of((at // self.bands) * self.width, self.width), self.width)

    def band(self, at):
        return row_block(lax.rem(at, self.bands) * self.height, self.height)

    def chunk_rows(self, h, at):
        start = h * HD + self.core * (HD // 2) + self.far * (HD // 4)
        return row_block(start + lax.rem(at, self.bands) * self.height, self.height)

    def copy(self, kind, h, src, dst, peer):
        return pltpu.make_async_remote_copy(
            src_ref=src, dst_ref=dst, send_sem=self.sems.at[0, kind, h],
            recv_sem=self.sems.at[1, kind, h], device_id={"ctx": peer}, device_id_type=MESH)

    def dp_copy(self, kind, h, step, src, dst):
        return pltpu.make_async_remote_copy(
            src_ref=src, dst_ref=dst, send_sem=self.dp_sems.at[0, kind, h, step - 1],
            recv_sem=self.dp_sems.at[1, kind, h, step - 1],
            device_id={"dp": lax.rem(self.dp_at + step, self.n_dp)}, device_id_type=MESH)

    def core_rows(self, h, core):
        return row_block(h * HD + core * (HD // 2), HD // 2)

    def far_rows(self, h, far):
        return row_block(h * HD + self.core * (HD // 2) + far * (HD // 4), HD // 4)

    def reduce1(self, h):
        return self.copy(0, h, self.part.at[self.core_rows(h, 1 - self.core)], self.in1.at[h],
                         self.core_peer)

    def reduce2(self, h):
        return self.copy(1, h, self.sum1.at[h, row_block((1 - self.far) * (HD // 4), HD // 4)],
                         self.in2.at[h], self.far_peer)

    def reduce3(self, h, step):
        peer = lax.rem(self.dp_at + step, self.n_dp)
        return self.dp_copy(0, h, step, self.sum2.at[h, self.band(peer), self.cols(peer)],
                            self.in3.at[h, step - 1])

    def share1(self, h, step, owner):
        return self.dp_copy(1, h, step, self.final.at[h],
                            self.out.at[self.chunk_rows(h, owner), self.cols(owner)])

    def own_copy(self, h):
        return pltpu.make_async_copy(
            self.final.at[h], self.out.at[self.chunk_rows(h, self.dp_at), self.cols(self.dp_at)],
            self.own_sem.at[h])

    def share2(self, h, far):
        rows = self.far_rows(h, far)
        return self.copy(2, h, self.out.at[rows], self.out.at[rows], self.far_peer)

    def share3(self, h, core):
        rows = self.core_rows(h, core)
        return self.copy(3, h, self.out.at[rows], self.out.at[rows], self.core_peer)

    def step0(self, h):
        self.reduce1(h).start()

    def step1(self, h):
        self.reduce1(h).wait_recv()
        mine = self.part[self.core_rows(h, self.core), :].astype(jnp.float32)
        self.sum1[h] = (mine + self.in1[h].astype(jnp.float32)).astype(jnp.bfloat16)
        self.reduce2(h).start()

    def step2(self, h):
        self.reduce2(h).wait_recv()
        mine = self.sum1[h, row_block(self.far * (HD // 4), HD // 4), :].astype(jnp.float32)
        self.sum2[h] = (mine + self.in2[h].astype(jnp.float32)).astype(jnp.bfloat16)
        for step in range(1, self.n_dp):
            self.reduce3(h, step).start()

    def step3(self, h):
        total = self.sum2[h, self.band(self.dp_at), self.cols(self.dp_at)].astype(jnp.float32)
        for step in range(1, self.n_dp):
            self.reduce3(h, step).wait_recv()
            total = total + self.in3[h, step - 1].astype(jnp.float32)
        self.final[h] = (total / self.n_dp).astype(jnp.bfloat16)
        self.own_copy(h).start()
        for step in range(1, self.n_dp):
            self.share1(h, step, self.dp_at).start()

    def step4(self, h):
        self.own_copy(h).wait()
        for step in range(1, self.n_dp):
            self.share1(h, step, lax.rem(self.dp_at + self.n_dp - step, self.n_dp)).wait_recv()
        self.share2(h, self.far).start()

    def step5(self, h):
        self.share2(h, 1 - self.far).wait_recv()
        self.share3(h, self.core).start()

    def finish(self, h):
        self.share3(h, 1 - self.core).wait_recv()
        self.share3(h, self.core).wait_send()
        self.share2(h, self.far).wait_send()
        self.reduce1(h).wait_send()
        self.reduce2(h).wait_send()
        for step in range(1, self.n_dp):
            self.reduce3(h, step).wait_send()
            self.share1(h, step, self.dp_at).wait_send()


def out_kernel(n_dp, n_uly, n_ctx, heads, dqh, own, edge, wpart, dq, dk, dv, wout,
               inbox, low, own_sem, send_sem, recv_sem, halo_send, halo_recv, *weight_refs):
    uly_at, ctx_at = lax.axis_index("uly"), lax.axis_index("ctx")
    rows = dq.shape[0]
    weight = WeightSum(n_dp, wpart, wout, *weight_refs)
    greet_groups((("uly", n_uly), ("ctx", n_ctx), ("dp", n_dp)))

    def source(h, i):
        return dqh.at[h] if i == 2 else low.at[h, i]

    targets = (dk, dv, dq)

    def piece(h, i, step, owner):
        peer = lax.rem(uly_at + step, n_uly)
        return pltpu.make_async_remote_copy(
            src_ref=source(h, i).at[row_block(peer * rows, rows)],
            dst_ref=targets[i].at[:, head_cols(owner * heads + h)],
            send_sem=send_sem.at[h, i, step - 1],
            recv_sem=recv_sem.at[h, i, step - 1],
            device_id={"uly": peer}, device_id_type=MESH)

    def own_piece(h, i):
        return pltpu.make_async_copy(
            source(h, i).at[row_block(uly_at * rows, rows)],
            targets[i].at[:, head_cols(uly_at * heads + h)], own_sem.at[h, i])

    def halo(h, side):
        return pltpu.make_async_remote_copy(
            src_ref=edge.at[h, side],
            dst_ref=inbox.at[h, 1 - side],
            send_sem=halo_send.at[h, side],
            recv_sem=halo_recv.at[h, side],
            device_id={"ctx": ctx_at - 1 if side == 0 else ctx_at + 1}, device_id_type=MESH)

    def send_out(h, i):
        for step in range(1, n_uly):
            piece(h, i, step, uly_at).start()
        own_piece(h, i).start()

    for h in range(heads):
        @pl.when(ctx_at > 0)
        def _():
            halo(h, 0).start()

        @pl.when(ctx_at < n_ctx - 1)
        def _():
            halo(h, 1).start()

    for h in range(heads):
        weight.step0(h)
    for h in range(heads):
        send_out(h, 2)
    for h in range(heads):
        @pl.when(ctx_at == 0)
        def _():
            halo(h, 0).wait_recv()
            low[h] = (own[h] + inbox[h, 1].astype(jnp.float32)).astype(jnp.bfloat16)

        @pl.when(ctx_at == n_ctx - 1)
        def _():
            halo(h, 1).wait_recv()
            low[h] = (own[h] + inbox[h, 0].astype(jnp.float32)).astype(jnp.bfloat16)

        @pl.when(jnp.logical_and(ctx_at > 0, ctx_at < n_ctx - 1))
        def _():
            halo(h, 0).wait_recv()
            halo(h, 1).wait_recv()
            both = inbox[h, 0].astype(jnp.float32) + inbox[h, 1].astype(jnp.float32)
            low[h] = (own[h] + both).astype(jnp.bfloat16)

        for i in range(2):
            send_out(h, i)
        weight.step1(h)
    stages = (weight.step2, weight.step3, weight.step4, weight.step5)
    for at in range(heads + len(stages) - 1):
        for lag, stage in enumerate(stages):
            if 0 <= at - lag < heads:
                stage(at - lag)
    for h in range(heads):
        weight.finish(h)
    for h in range(heads):
        for i in range(3):
            for step in range(1, n_uly):
                owner = lax.rem(uly_at + n_uly - step, n_uly)
                piece(h, i, step, owner).wait_recv()
                piece(h, i, step, uly_at).wait_send()
            own_piece(h, i).wait()

        @pl.when(ctx_at > 0)
        def _():
            halo(h, 0).wait_send()

        @pl.when(ctx_at < n_ctx - 1)
        def _():
            halo(h, 1).wait_send()


def scatter_tokens(dqh, own, edge, wpart, rows, n_dp, n_uly, n_ctx, heads):
    anywhere = pl.BlockSpec(memory_space=pl.ANY)
    dout = wpart.shape[1]
    _, height, width = chunk_of(n_dp, dout)
    shape = jax.ShapeDtypeStruct((rows, n_uly * heads * HD), jnp.bfloat16)
    return pl.pallas_call(
        functools.partial(out_kernel, n_dp, n_uly, n_ctx, heads),
        out_shape=(shape,) * 3 + (jax.ShapeDtypeStruct(wpart.shape, jnp.bfloat16),),
        in_specs=[anywhere, pl.BlockSpec(memory_space=pltpu.VMEM), anywhere,
                  pl.BlockSpec(memory_space=pltpu.VMEM)],
        out_specs=(anywhere,) * 4,
        scratch_shapes=[
            pltpu.VMEM((heads, 2, 2, LAYER, HD), jnp.bfloat16),
            pltpu.VMEM((heads, 2, LAYER, HD), jnp.bfloat16),
            pltpu.SemaphoreType.DMA((heads, 3)),
            pltpu.SemaphoreType.DMA((heads, 3, n_uly - 1)),
            pltpu.SemaphoreType.DMA((heads, 3, n_uly - 1)),
            pltpu.SemaphoreType.DMA((heads, 2)),
            pltpu.SemaphoreType.DMA((heads, 2)),
            pltpu.VMEM((heads, HD // 2, dout), jnp.bfloat16),
            pltpu.VMEM((heads, HD // 2, dout), jnp.bfloat16),
            pltpu.VMEM((heads, HD // 4, dout), jnp.bfloat16),
            pltpu.VMEM((heads, HD // 4, dout), jnp.bfloat16),
            pltpu.VMEM((heads, n_dp - 1, height, width), jnp.bfloat16),
            pltpu.VMEM((heads, height, width), jnp.bfloat16),
            pltpu.SemaphoreType.DMA((2, 4, heads)),
            pltpu.SemaphoreType.DMA((2, 2, heads, n_dp - 1)),
            pltpu.SemaphoreType.DMA((heads,)),
        ],
        compiler_params=pltpu.CompilerParams(
            collective_id=1, has_side_effects=True, vmem_limit_bytes=VMEM_LIMIT),
        name="scatter_tokens",
    )(dqh, own, edge, wpart)


def allowed_tiles(tile_lists, windows, heads):
    ctx_at, uly_at = lax.axis_index("ctx"), lax.axis_index("uly")
    listed = lax.dynamic_slice_in_dim(tile_lists, ctx_at * TW, TW, 0) >= 0
    reach = lax.dynamic_slice_in_dim(windows, uly_at * heads, heads, 0)
    slot_ids = jnp.arange(SLOTS, dtype=jnp.int32)
    spot_ids = jnp.arange(TW, dtype=jnp.int32)
    near_time = jnp.abs(slot_ids // TW - 1)[None, :] <= reach[:, 0:1]
    far = jnp.abs(slot_ids[None, :] % TW - spot_ids[:, None])
    near_space = far[None] <= reach[:, 1][:, None, None]
    allowed = listed[None] & near_time[:, None, :] & near_space
    return allowed.astype(jnp.int32).reshape(-1)


def on_device(queries, key_rows, value_rows, out_grad, out_weight, tile_lists, windows):
    n_uly, n_ctx = lax.axis_size("uly"), lax.axis_size("ctx")
    heads = HEADS // n_uly
    rows = queries.shape[1]
    qh, kw, vw, g = gather_heads(
        queries[0], key_rows[0], value_rows[0], out_grad[0], out_weight, n_uly, n_ctx, heads)
    allow = allowed_tiles(tile_lists, windows, heads)
    dqh, own, edge, wpart = attend(allow, qh, kw, vw, g, out_grad[0], heads)
    dq, dk, dv, weight_grad = scatter_tokens(
        dqh, own, edge, wpart, rows, lax.axis_size("dp"), n_uly, n_ctx, heads)
    return (dq[None], dk[None], dv[None], weight_grad)


def solution(mesh):
    tokens = P("dp", ("ctx", "uly"), None)
    in_specs = (tokens, tokens, tokens, P("dp", "ctx", None), P("uly", None), P(), P())
    out_specs = (tokens, tokens, tokens, P("uly", None))
    return jax.shard_map(
        on_device, mesh=mesh, in_specs=in_specs, out_specs=out_specs, check_vma=False
    )
```

```python
import functools

import jax
import jax.numpy as jnp
from jax import lax
from jax.experimental import pallas as pl
from jax.experimental.pallas import tpu as pltpu
from jax.sharding import PartitionSpec as P

HEADS = 12
HD = 128
TILE = 384
TW = 2
SLOTS = 3 * TW
LAYER = TW * TILE
MESH = pl.DeviceIdType.MESH
LOG2E = 1.4426950408889634
VMEM_LIMIT = 56 * 1024 * 1024


def head_cols(at):
    return pl.ds(pl.multiple_of(at * HD, HD), HD)


def row_block(start, rows):
    return pl.ds(pl.multiple_of(start, rows), rows)


def greet(n_uly, n_ctx, uly_at, ctx_at):
    barrier = pltpu.get_barrier_semaphore()
    for step in range(1, n_uly):
        peer = lax.rem(uly_at + step, n_uly)
        pl.semaphore_signal(barrier, inc=1, device_id={"uly": peer}, device_id_type=MESH)

    @pl.when(ctx_at > 0)
    def _():
        pl.semaphore_signal(barrier, inc=1, device_id={"ctx": ctx_at - 1}, device_id_type=MESH)

    @pl.when(ctx_at < n_ctx - 1)
    def _():
        pl.semaphore_signal(barrier, inc=1, device_id={"ctx": ctx_at + 1}, device_id_type=MESH)

    interior = jnp.logical_and(ctx_at > 0, ctx_at < n_ctx - 1)
    pl.semaphore_wait(barrier, n_uly + interior.astype(jnp.int32))


def greet_groups(sizes):
    barrier = pltpu.get_barrier_semaphore()
    for axis, count in sizes:
        at = lax.axis_index(axis)
        for step in range(1, count):
            pl.semaphore_signal(barrier, inc=1, device_id={axis: lax.rem(at + step, count)},
                                device_id_type=MESH)
    pl.semaphore_wait(barrier, sum(count - 1 for _, count in sizes))


def in_kernel(n_uly, n_ctx, heads, q, k, v, og, ow, qh, kw, vw, g,
              og_v, ow_v, load_sem, own_sem, send_sem, recv_sem, halo_send, halo_recv):
    uly_at, ctx_at = lax.axis_index("uly"), lax.axis_index("ctx")
    rows = q.shape[0]
    loads = [pltpu.make_async_copy(og, og_v, load_sem.at[0]),
             pltpu.make_async_copy(ow, ow_v, load_sem.at[1])]
    for load in loads:
        load.start()
    triples = ((k, kw, LAYER), (v, vw, LAYER), (q, qh, 0))
    own = {}
    for h in range(heads):
        for i, (src, dst, base) in enumerate(triples):
            own[h, i] = pltpu.make_async_copy(
                src.at[:, head_cols(uly_at * heads + h)],
                dst.at[h, row_block(base + uly_at * rows, rows)],
                own_sem.at[h, i])
            own[h, i].start()
    greet(n_uly, n_ctx, uly_at, ctx_at)

    def piece(h, i, step, owner):
        src, dst, base = triples[i]
        peer = lax.rem(uly_at + step, n_uly)
        return pltpu.make_async_remote_copy(
            src_ref=src.at[:, head_cols(peer * heads + h)],
            dst_ref=dst.at[h, row_block(base + owner * rows, rows)],
            send_sem=send_sem.at[h, i, step - 1],
            recv_sem=recv_sem.at[h, i, step - 1],
            device_id={"uly": peer}, device_id_type=MESH)

    order = [(h, i) for h in range(heads) for i in range(2)] + [(h, 2) for h in range(heads)]
    for h, i in order:
        for step in range(1, n_uly):
            piece(h, i, step, uly_at).start()

    for load in loads:
        load.wait()

    def grad_rows(at, carry):
        chunk = row_block(at * TILE, TILE)
        out = lax.dot_general(og_v[chunk, :], ow_v[...], (((1,), (1,)), ((), ())),
                              preferred_element_type=jnp.float32).astype(jnp.bfloat16)
        for h in range(heads):
            g[h, chunk, :] = out[:, h * HD:(h + 1) * HD]
        return carry

    lax.fori_loop(0, TW, grad_rows, 0)

    def arrived(h, i):
        own[h, i].wait()
        for step in range(1, n_uly):
            owner = lax.rem(uly_at + n_uly - step, n_uly)
            piece(h, i, step, owner).wait_recv()

    def halo(h, i, side):
        buf = triples[i][1]
        slot = 2 if side == 0 else 0
        return pltpu.make_async_remote_copy(
            src_ref=buf.at[h, pl.ds(LAYER, LAYER)],
            dst_ref=buf.at[h, pl.ds(slot * LAYER, LAYER)],
            send_sem=halo_send.at[h, i, side],
            recv_sem=halo_recv.at[h, i, side],
            device_id={"ctx": ctx_at - 1 if side == 0 else ctx_at + 1}, device_id_type=MESH)

    for h in range(heads):
        for i in range(2):
            arrived(h, i)

            @pl.when(ctx_at > 0)
            def _():
                halo(h, i, 0).start()

            @pl.when(ctx_at < n_ctx - 1)
            def _():
                halo(h, i, 1).start()

    for h in range(heads):
        arrived(h, 2)
    for h in range(heads):
        for i in range(2):
            @pl.when(ctx_at > 0)
            def _():
                halo(h, i, 0).wait_send()
                halo(h, i, 1).wait_recv()

            @pl.when(ctx_at < n_ctx - 1)
            def _():
                halo(h, i, 1).wait_send()
                halo(h, i, 0).wait_recv()
    for h, i in order:
        for step in range(1, n_uly):
            piece(h, i, step, uly_at).wait_send()


def gather_heads(q, k, v, og, ow, n_uly, n_ctx, heads):
    span = LAYER
    anywhere = pl.BlockSpec(memory_space=pl.ANY)
    return pl.pallas_call(
        functools.partial(in_kernel, n_uly, n_ctx, heads),
        out_shape=(jax.ShapeDtypeStruct((heads, span, HD), jnp.bfloat16),
                   jax.ShapeDtypeStruct((heads, 3 * span, HD), jnp.bfloat16),
                   jax.ShapeDtypeStruct((heads, 3 * span, HD), jnp.bfloat16),
                   jax.ShapeDtypeStruct((heads, span, HD), jnp.bfloat16)),
        in_specs=[anywhere] * 5,
        out_specs=(anywhere, anywhere, anywhere, pl.BlockSpec(memory_space=pltpu.VMEM)),
        scratch_shapes=[
            pltpu.VMEM(og.shape, jnp.bfloat16),
            pltpu.VMEM(ow.shape, jnp.bfloat16),
            pltpu.SemaphoreType.DMA((2,)),
            pltpu.SemaphoreType.DMA((heads, 3)),
            pltpu.SemaphoreType.DMA((heads, 3, n_uly - 1)),
            pltpu.SemaphoreType.DMA((heads, 3, n_uly - 1)),
            pltpu.SemaphoreType.DMA((heads, 2, 2)),
            pltpu.SemaphoreType.DMA((heads, 2, 2)),
        ],
        compiler_params=pltpu.CompilerParams(
            collective_id=0, has_side_effects=True, vmem_limit_bytes=24 * 1024 * 1024),
        name="gather_heads",
    )(q, k, v, og, ow)


def lane_fold(x, op):
    out = x[:, 0:HD]
    for at in range(HD, x.shape[1], HD):
        out = op(out, x[:, at:at + HD])
    return out


def attend_kernel(allow, q, kw, vw, g, og, dq, own, edge, wpart,
                  s_buf, p_buf, m_buf, l_buf, o_buf, dq_buf, dk_buf, dv_buf, att):
    head = pl.program_id(0)
    scaling = HD ** (-0.5)
    dk_buf[...] = jnp.zeros_like(dk_buf)
    dv_buf[...] = jnp.zeros_like(dv_buf)
    nt = (((1,), (1,)), ((), ()))
    tn = (((0,), (0,)), ((), ()))

    def query_tile(spot, carry):
        rows = row_block(spot * TILE, TILE)
        flags = (head * TW + spot) * SLOTS

        def each(body):
            def step(slot, c):
                @pl.when(allow[flags + slot] > 0)
                def _():
                    body(slot, row_block(slot * TILE, TILE))
                return c
            lax.fori_loop(0, SLOTS, step, 0)

        m_buf[...] = jnp.full_like(m_buf, -jnp.inf)
        l_buf[...] = jnp.zeros_like(l_buf)
        o_buf[...] = jnp.zeros_like(o_buf)
        dq_buf[...] = jnp.zeros_like(dq_buf)

        def score(slot, keys):
            s = lax.dot_general(q[0, rows, :], kw[0, keys, :], nt, preferred_element_type=jnp.float32)
            s_buf[slot] = s
            m_buf[...] = jnp.maximum(m_buf[...], lane_fold(s, jnp.maximum))

        each(score)
        top = jnp.max(m_buf[...], axis=1, keepdims=True)

        def weigh(slot, keys):
            p = jnp.exp2((s_buf[slot] - top) * (scaling * LOG2E))
            l_buf[...] += lane_fold(p, jnp.add)
            low = p.astype(jnp.bfloat16)
            p_buf[slot] = low
            o_buf[...] += jnp.dot(low, vw[0, keys, :], preferred_element_type=jnp.float32)

        each(weigh)
        inv = 1.0 / jnp.sum(l_buf[...], axis=1, keepdims=True)
        out = o_buf[...] * inv
        att[rows, :] = out.astype(jnp.bfloat16)
        gp = (g[0, rows, :].astype(jnp.float32) * inv).astype(jnp.bfloat16)
        delta = jnp.sum(out * gp.astype(jnp.float32), axis=1, keepdims=True)

        def back(slot, keys):
            low = p_buf[slot]
            dp = lax.dot_general(gp, vw[0, keys, :], nt, preferred_element_type=jnp.float32)
            ds = low * (dp - delta).astype(jnp.bfloat16)
            dv_buf[keys, :] += lax.dot_general(low, gp, tn, preferred_element_type=jnp.float32)
            dk_buf[keys, :] += lax.dot_general(ds, q[0, rows, :], tn, preferred_element_type=jnp.float32)
            dq_buf[...] += jnp.dot(ds, kw[0, keys, :], preferred_element_type=jnp.float32)

        each(back)
        dq[0, rows, :] = (dq_buf[...] * scaling).astype(jnp.bfloat16)
        return carry

    lax.fori_loop(0, TW, query_tile, 0)
    own[0, 0] = dk_buf[LAYER:2 * LAYER, :] * scaling
    own[0, 1] = dv_buf[LAYER:2 * LAYER, :]
    for side in range(2):
        part = slice(2 * side * LAYER, (2 * side + 1) * LAYER)
        edge[0, side, 0] = (dk_buf[part, :] * scaling).astype(jnp.bfloat16)
        edge[0, side, 1] = dv_buf[part, :].astype(jnp.bfloat16)
    width = 2 * TILE

    def weight_cols(at, carry):
        cols = row_block(at * width, width)
        wpart[:, cols] = lax.dot_general(
            att[...], og[:, cols], tn, preferred_element_type=jnp.float32).astype(wpart.dtype)
        return carry

    lax.fori_loop(0, og.shape[1] // width, weight_cols, 0)


def attend(allow, q, kw, vw, g, og, heads):
    def per_head(*dims):
        return pl.BlockSpec((1,) + dims, lambda h, allow: (h,) + (0,) * len(dims))

    dout = og.shape[1]
    grid_spec = pltpu.PrefetchScalarGridSpec(
        num_scalar_prefetch=1,
        grid=(heads,),
        in_specs=[per_head(LAYER, HD), per_head(3 * LAYER, HD), per_head(3 * LAYER, HD),
                  per_head(LAYER, HD), pl.BlockSpec((LAYER, dout), lambda h, allow: (0, 0))],
        out_specs=[per_head(LAYER, HD), per_head(2, LAYER, HD), per_head(2, 2, LAYER, HD),
                   pl.BlockSpec((HD, dout), lambda h, allow: (h, 0))],
        scratch_shapes=[
            pltpu.VMEM((SLOTS, TILE, TILE), jnp.float32),
            pltpu.VMEM((SLOTS, TILE, TILE), jnp.bfloat16),
            pltpu.VMEM((TILE, HD), jnp.float32),
            pltpu.VMEM((TILE, HD), jnp.float32),
            pltpu.VMEM((TILE, HD), jnp.float32),
            pltpu.VMEM((TILE, HD), jnp.float32),
            pltpu.VMEM((3 * LAYER, HD), jnp.float32),
            pltpu.VMEM((3 * LAYER, HD), jnp.float32),
            pltpu.VMEM((LAYER, HD), jnp.bfloat16),
        ])
    return pl.pallas_call(
        attend_kernel,
        out_shape=(jax.ShapeDtypeStruct((heads, LAYER, HD), jnp.bfloat16),
                   jax.ShapeDtypeStruct((heads, 2, LAYER, HD), jnp.float32),
                   jax.ShapeDtypeStruct((heads, 2, 2, LAYER, HD), jnp.bfloat16),
                   jax.ShapeDtypeStruct((heads * HD, dout), jnp.bfloat16)),
        grid_spec=grid_spec,
        compiler_params=pltpu.CompilerParams(vmem_limit_bytes=VMEM_LIMIT),
        name="attend",
    )(allow, q, kw, vw, g, og)


def chunk_of(n_dp, dout):
    bands = 1 if (dout // n_dp) % 128 == 0 else 2
    return bands, HD // 4 // bands, dout * bands // n_dp


class WeightSum:
    def __init__(self, n_dp, part, out, in1, sum1, in2, sum2, in3, final, sems, dp_sems, own_sem):
        self.n_dp, self.part, self.out = n_dp, part, out
        self.in1, self.sum1, self.in2, self.sum2, self.in3, self.final = in1, sum1, in2, sum2, in3, final
        self.sems, self.dp_sems, self.own_sem = sems, dp_sems, own_sem
        ctx_at = lax.axis_index("ctx")
        self.dp_at = lax.axis_index("dp")
        self.core, self.far = lax.rem(ctx_at, 2), ctx_at // 2
        self.core_peer = ctx_at + 1 - 2 * self.core
        self.far_peer = lax.rem(ctx_at + 2, 4)
        self.bands, self.height, self.width = chunk_of(n_dp, part.shape[1])

    def cols(self, at):
        return pl.ds(pl.multiple_of((at // self.bands) * self.width, self.width), self.width)

    def band(self, at):
        return row_block(lax.rem(at, self.bands) * self.height, self.height)

    def chunk_rows(self, h, at):
        start = h * HD + self.core * (HD // 2) + self.far * (HD // 4)
        return row_block(start + lax.rem(at, self.bands) * self.height, self.height)

    def copy(self, kind, h, src, dst, peer):
        return pltpu.make_async_remote_copy(
            src_ref=src, dst_ref=dst, send_sem=self.sems.at[0, kind, h],
            recv_sem=self.sems.at[1, kind, h], device_id={"ctx": peer}, device_id_type=MESH)

    def dp_copy(self, kind, h, step, src, dst):
        return pltpu.make_async_remote_copy(
            src_ref=src, dst_ref=dst, send_sem=self.dp_sems.at[0, kind, h, step - 1],
            recv_sem=self.dp_sems.at[1, kind, h, step - 1],
            device_id={"dp": lax.rem(self.dp_at + step, self.n_dp)}, device_id_type=MESH)

    def core_rows(self, h, core):
        return row_block(h * HD + core * (HD // 2), HD // 2)

    def far_rows(self, h, far):
        return row_block(h * HD + self.core * (HD // 2) + far * (HD // 4), HD // 4)

    def reduce1(self, h):
        return self.copy(0, h, self.part.at[self.core_rows(h, 1 - self.core)], self.in1.at[h],
                         self.core_peer)

    def reduce2(self, h):
        return self.copy(1, h, self.sum1.at[h, row_block((1 - self.far) * (HD // 4), HD // 4)],
                         self.in2.at[h], self.far_peer)

    def reduce3(self, h, step):
        peer = lax.rem(self.dp_at + step, self.n_dp)
        return self.dp_copy(0, h, step, self.sum2.at[h, self.band(peer), self.cols(peer)],
                            self.in3.at[h, step - 1])

    def share1(self, h, step, owner):
        return self.dp_copy(1, h, step, self.final.at[h],
                            self.out.at[self.chunk_rows(h, owner), self.cols(owner)])

    def own_copy(self, h):
        return pltpu.make_async_copy(
            self.final.at[h], self.out.at[self.chunk_rows(h, self.dp_at), self.cols(self.dp_at)],
            self.own_sem.at[h])

    def share2(self, h, far):
        rows = self.far_rows(h, far)
        return self.copy(2, h, self.out.at[rows], self.out.at[rows], self.far_peer)

    def share3(self, h, core):
        rows = self.core_rows(h, core)
        return self.copy(3, h, self.out.at[rows], self.out.at[rows], self.core_peer)

    def step0(self, h):
        self.reduce1(h).start()

    def step1(self, h):
        self.reduce1(h).wait_recv()
        mine = self.part[self.core_rows(h, self.core), :].astype(jnp.float32)
        self.sum1[h] = (mine + self.in1[h].astype(jnp.float32)).astype(jnp.bfloat16)
        self.reduce2(h).start()

    def step2(self, h):
        self.reduce2(h).wait_recv()
        mine = self.sum1[h, row_block(self.far * (HD // 4), HD // 4), :].astype(jnp.float32)
        self.sum2[h] = (mine + self.in2[h].astype(jnp.float32)).astype(jnp.bfloat16)
        for step in range(1, self.n_dp):
            self.reduce3(h, step).start()

    def step3(self, h):
        total = self.sum2[h, self.band(self.dp_at), self.cols(self.dp_at)].astype(jnp.float32)
        for step in range(1, self.n_dp):
            self.reduce3(h, step).wait_recv()
            total = total + self.in3[h, step - 1].astype(jnp.float32)
        self.final[h] = (total / self.n_dp).astype(jnp.bfloat16)
        self.own_copy(h).start()
        for step in range(1, self.n_dp):
            self.share1(h, step, self.dp_at).start()

    def step4(self, h):
        self.own_copy(h).wait()
        for step in range(1, self.n_dp):
            self.share1(h, step, lax.rem(self.dp_at + self.n_dp - step, self.n_dp)).wait_recv()
        self.share2(h, self.far).start()

    def step5(self, h):
        self.share2(h, 1 - self.far).wait_recv()
        self.share3(h, self.core).start()

    def finish(self, h):
        self.share3(h, 1 - self.core).wait_recv()
        self.share3(h, self.core).wait_send()
        self.share2(h, self.far).wait_send()
        self.reduce1(h).wait_send()
        self.reduce2(h).wait_send()
        for step in range(1, self.n_dp):
            self.reduce3(h, step).wait_send()
            self.share1(h, step, self.dp_at).wait_send()


def out_kernel(n_dp, n_uly, n_ctx, heads, dqh, own, edge, wpart, dq, dk, dv, wout,
               inbox, low, own_sem, send_sem, recv_sem, halo_send, halo_recv, *weight_refs):
    uly_at, ctx_at = lax.axis_index("uly"), lax.axis_index("ctx")
    rows = dq.shape[0]
    weight = WeightSum(n_dp, wpart, wout, *weight_refs)
    greet_groups((("uly", n_uly), ("ctx", n_ctx), ("dp", n_dp)))

    def source(h, i):
        return dqh.at[h] if i == 2 else low.at[h, i]

    targets = (dk, dv, dq)

    def piece(h, i, step, owner):
        peer = lax.rem(uly_at + step, n_uly)
        return pltpu.make_async_remote_copy(
            src_ref=source(h, i).at[row_block(peer * rows, rows)],
            dst_ref=targets[i].at[:, head_cols(owner * heads + h)],
            send_sem=send_sem.at[h, i, step - 1],
            recv_sem=recv_sem.at[h, i, step - 1],
            device_id={"uly": peer}, device_id_type=MESH)

    def own_piece(h, i):
        return pltpu.make_async_copy(
            source(h, i).at[row_block(uly_at * rows, rows)],
            targets[i].at[:, head_cols(uly_at * heads + h)], own_sem.at[h, i])

    def halo(h, side):
        return pltpu.make_async_remote_copy(
            src_ref=edge.at[h, side],
            dst_ref=inbox.at[h, 1 - side],
            send_sem=halo_send.at[h, side],
            recv_sem=halo_recv.at[h, side],
            device_id={"ctx": ctx_at - 1 if side == 0 else ctx_at + 1}, device_id_type=MESH)

    def send_out(h, i):
        for step in range(1, n_uly):
            piece(h, i, step, uly_at).start()
        own_piece(h, i).start()

    for h in range(heads):
        @pl.when(ctx_at > 0)
        def _():
            halo(h, 0).start()

        @pl.when(ctx_at < n_ctx - 1)
        def _():
            halo(h, 1).start()

    for h in range(heads):
        weight.step0(h)
    for h in range(heads):
        send_out(h, 2)
    for h in range(heads):
        weight.step1(h)
    for h in range(heads):
        @pl.when(ctx_at == 0)
        def _():
            halo(h, 0).wait_recv()
            low[h] = (own[h] + inbox[h, 1].astype(jnp.float32)).astype(jnp.bfloat16)

        @pl.when(ctx_at == n_ctx - 1)
        def _():
            halo(h, 1).wait_recv()
            low[h] = (own[h] + inbox[h, 0].astype(jnp.float32)).astype(jnp.bfloat16)

        @pl.when(jnp.logical_and(ctx_at > 0, ctx_at < n_ctx - 1))
        def _():
            halo(h, 0).wait_recv()
            halo(h, 1).wait_recv()
            both = inbox[h, 0].astype(jnp.float32) + inbox[h, 1].astype(jnp.float32)
            low[h] = (own[h] + both).astype(jnp.bfloat16)

        for i in range(2):
            send_out(h, i)
    stages = (weight.step2, weight.step3, weight.step4, weight.step5)
    for at in range(heads + len(stages) - 1):
        for lag, stage in enumerate(stages):
            if 0 <= at - lag < heads:
                stage(at - lag)
    for h in range(heads):
        weight.finish(h)
    for h in range(heads):
        for i in range(3):
            for step in range(1, n_uly):
                owner = lax.rem(uly_at + n_uly - step, n_uly)
                piece(h, i, step, owner).wait_recv()
                piece(h, i, step, uly_at).wait_send()
            own_piece(h, i).wait()

        @pl.when(ctx_at > 0)
        def _():
            halo(h, 0).wait_send()

        @pl.when(ctx_at < n_ctx - 1)
        def _():
            halo(h, 1).wait_send()


def scatter_tokens(dqh, own, edge, wpart, rows, n_dp, n_uly, n_ctx, heads):
    anywhere = pl.BlockSpec(memory_space=pl.ANY)
    dout = wpart.shape[1]
    _, height, width = chunk_of(n_dp, dout)
    shape = jax.ShapeDtypeStruct((rows, n_uly * heads * HD), jnp.bfloat16)
    return pl.pallas_call(
        functools.partial(out_kernel, n_dp, n_uly, n_ctx, heads),
        out_shape=(shape,) * 3 + (jax.ShapeDtypeStruct(wpart.shape, jnp.bfloat16),),
        in_specs=[anywhere, pl.BlockSpec(memory_space=pltpu.VMEM), anywhere,
                  pl.BlockSpec(memory_space=pltpu.VMEM)],
        out_specs=(anywhere,) * 4,
        scratch_shapes=[
            pltpu.VMEM((heads, 2, 2, LAYER, HD), jnp.bfloat16),
            pltpu.VMEM((heads, 2, LAYER, HD), jnp.bfloat16),
            pltpu.SemaphoreType.DMA((heads, 3)),
            pltpu.SemaphoreType.DMA((heads, 3, n_uly - 1)),
            pltpu.SemaphoreType.DMA((heads, 3, n_uly - 1)),
            pltpu.SemaphoreType.DMA((heads, 2)),
            pltpu.SemaphoreType.DMA((heads, 2)),
            pltpu.VMEM((heads, HD // 2, dout), jnp.bfloat16),
            pltpu.VMEM((heads, HD // 2, dout), jnp.bfloat16),
            pltpu.VMEM((heads, HD // 4, dout), jnp.bfloat16),
            pltpu.VMEM((heads, HD // 4, dout), jnp.bfloat16),
            pltpu.VMEM((heads, n_dp - 1, height, width), jnp.bfloat16),
            pltpu.VMEM((heads, height, width), jnp.bfloat16),
            pltpu.SemaphoreType.DMA((2, 4, heads)),
            pltpu.SemaphoreType.DMA((2, 2, heads, n_dp - 1)),
            pltpu.SemaphoreType.DMA((heads,)),
        ],
        compiler_params=pltpu.CompilerParams(
            collective_id=1, has_side_effects=True, vmem_limit_bytes=24 * 1024 * 1024),
        name="scatter_tokens",
    )(dqh, own, edge, wpart)


def allowed_tiles(tile_lists, windows, heads):
    ctx_at, uly_at = lax.axis_index("ctx"), lax.axis_index("uly")
    listed = lax.dynamic_slice_in_dim(tile_lists, ctx_at * TW, TW, 0) >= 0
    reach = lax.dynamic_slice_in_dim(windows, uly_at * heads, heads, 0)
    slot_ids = jnp.arange(SLOTS, dtype=jnp.int32)
    spot_ids = jnp.arange(TW, dtype=jnp.int32)
    near_time = jnp.abs(slot_ids // TW - 1)[None, :] <= reach[:, 0:1]
    far = jnp.abs(slot_ids[None, :] % TW - spot_ids[:, None])
    near_space = far[None] <= reach[:, 1][:, None, None]
    allowed = listed[None] & near_time[:, None, :] & near_space
    return allowed.astype(jnp.int32).reshape(-1)


def on_device(queries, key_rows, value_rows, out_grad, out_weight, tile_lists, windows):
    n_uly, n_ctx = lax.axis_size("uly"), lax.axis_size("ctx")
    heads = HEADS // n_uly
    rows = queries.shape[1]
    qh, kw, vw, g = gather_heads(
        queries[0], key_rows[0], value_rows[0], out_grad[0], out_weight, n_uly, n_ctx, heads)
    allow = allowed_tiles(tile_lists, windows, heads)
    dqh, own, edge, wpart = attend(allow, qh, kw, vw, g, out_grad[0], heads)
    dq, dk, dv, weight_grad = scatter_tokens(
        dqh, own, edge, wpart, rows, lax.axis_size("dp"), n_uly, n_ctx, heads)
    return (dq[None], dk[None], dv[None], weight_grad)


def solution(mesh):
    tokens = P("dp", ("ctx", "uly"), None)
    in_specs = (tokens, tokens, tokens, P("dp", "ctx", None), P("uly", None), P(), P())
    out_specs = (tokens, tokens, tokens, P("uly", None))
    return jax.shard_map(
        on_device, mesh=mesh, in_specs=in_specs, out_specs=out_specs, check_vma=False
    )
```
